512 devices in a mesh: replica: 32 (over z_hi, x, core), fsdp: 16 (over y, z_lo).
Axes of the slice: x: 4, y: 4, z: 16 (z_hi: 4, z_lo: 4; z = z_hi * 4 + z_lo), core: 2. Of those that a mesh axis runs over, the one named last changes fastest.
Arguments:
- activations: bfloat16 [32, 1, 2048, 4096], P('replica', None, 'fsdp'), may hold values from -6 to 6
- cotangent: bfloat16 [32, 1, 2048, 512], P('replica', None, 'fsdp'), may hold values from -6 to 6
- params: float32 [32, 4096, 512], P('replica', 'fsdp'), may hold values from -6 to 6
- first_moment: bfloat16 [32, 4096, 512], P('replica', 'fsdp'), may hold values from -3 to 3
- second_moment: float32 [32, 4096, 512], P('replica', 'fsdp'), may hold values from 0.01 to 1
- anchor: bfloat16 [4096, 512], P('fsdp'), may hold values from -6 to 6
- outer_momentum: bfloat16 [4096, 512], P('fsdp'), may hold values from -2 to 2
Outputs:
- merged: float32 [32, 4096, 512], P('replica', 'fsdp')
- new_first_moment: float32 [32, 4096, 512], P('replica', 'fsdp')
- input_grad: bfloat16 [32, 1, 2048, 4096], P('replica', None, 'fsdp')
The draws below stay inside these ranges and needn't reach their ends.
All inputs are finite; a program needn't handle non-finite values.
Results may differ from the reference program's by a relative error of at most 0.0049.
Values may be sent and summed in bfloat16 or wider, within the bound.
A program may use at most 64 MiB of HBM per device.

```python
import math
import jax
import jax.numpy as jnp
from jax import lax

D = 4096
KVW = 512
STEPS = 1
TOKR = 2048
REPLICAS = 32
N_REPLICA = 32


def with_spikes(result, rng, source, target, blocks, factor):
    owner, partner = [(jnp.arange(result.shape[position]) // (result.shape[position] // blocks)).reshape([-1 if axis == position else 1 for axis in range(result.ndim)]) for position in (source, target)]
    chosen = jax.random.permutation(rng, blocks)[partner]
    strong = (owner == chosen) | (owner == (partner + blocks // 2) % blocks)
    return jnp.where(strong, factor * result, result)


def levels(rng, extent, shards, smallest, largest):
    def one(axis_at, shards_of):
        heights = jax.random.uniform(jax.random.fold_in(jax.random.fold_in(rng, 6), axis_at), (shards_of,), jnp.float32, smallest / len(shards), largest / len(shards))
        return jnp.repeat(jnp.exp(heights), extent[axis_at] // shards_of).reshape((-1,) + (1,) * (len(extent) - axis_at - 1))

    level = one(*shards[0])
    for cut in shards[1:]:
        level = level * one(*cut)
    return level


def noise(stream_key, dims, width, reach, split=(), kind=jnp.bfloat16):
    values = width * jax.random.normal(stream_key, dims, jnp.float32)
    if split:
        values = values * levels(stream_key, dims, split, -0.22, 0.18)
    return jnp.clip(values, -reach, reach).astype(kind)


def heavy_noise(own_key, dims, spread, most, shards, heavy, dtype=jnp.bfloat16):
    drawn = spread * jax.random.normal(own_key, dims, jnp.float32)
    if shards:
        drawn = drawn * levels(own_key, dims, shards, -0.22, 0.18)
    return jnp.clip(with_spikes(drawn, jax.random.fold_in(own_key, 3), *heavy), -most, most).astype(dtype)


def setup_inputs(seed: int = 0) -> dict:
    streams_of = jax.random.split(jax.random.key(seed), 8)
    return {
        "activations": heavy_noise(streams_of[0], (REPLICAS, STEPS, TOKR, D), 1.0, 6.0, ((0, 32), (2, 16)), (2, 3, 16, 2.0)),
        "cotangent": noise(streams_of[1], (REPLICAS, STEPS, TOKR, KVW), 1.0, 6.0, ((0, 32), (2, 16))),
        "params": noise(streams_of[2], (REPLICAS, D, KVW), 1.0, 6.0, ((0, 32), (1, 16)), jnp.float32),
        "first_moment": noise(streams_of[3], (REPLICAS, D, KVW), 0.5, 3.0, ((0, 32), (1, 16))),
        "second_moment": jnp.clip(jnp.exp(math.log(1.0) - 4.6051702 * jax.random.uniform(streams_of[4], (REPLICAS, D, KVW), jnp.float32) ** levels(streams_of[4], (REPLICAS, D, KVW), ((0, 32), (1, 16)), -0.2, 0.2)), 0.01, 1.0),
        "anchor": noise(streams_of[5], (D, KVW), 1.0, 6.0, ((0, 16),)),
        "outer_momentum": noise(streams_of[6], (D, KVW), 0.3, 2.0, ((0, 16),)),
    }


BETA_FIRST = 0.9
BETA_SECOND = 0.95
EPSILON = 1e-08
WEIGHT_DECAY = 0.1
INNER_RATE = 0.03
OUTER_RATE = 0.7
OUTER_MOMENT = 0.9
MIXING = 0.5

def reference(activations, cotangent, params, first_moment, second_moment, anchor, outer_momentum):
    factor = jnp.float32(D) ** (-0.5)
    global_old = anchor.astype(jnp.float32)
    outer_delta = global_old[None] - params
    outer_grad = lax.optimization_barrier(jnp.sum(outer_delta, axis=0)) / N_REPLICA
    momentum_new = OUTER_MOMENT * outer_momentum.astype(jnp.float32) + outer_grad
    global_new = global_old - OUTER_RATE * (outer_grad + OUTER_MOMENT * momentum_new)

    def worker(bundle):
        inputs, upstream, weights, first_state, second = bundle
        first_state = first_state.astype(jnp.float32)
        results = []
        for inner_step in range(STEPS):
            scaled = (weights * factor).astype(jnp.bfloat16)
            results.append(jnp.dot(upstream[inner_step], scaled.T, preferred_element_type=jnp.float32).astype(jnp.bfloat16))
            gradient = jnp.dot(inputs[inner_step].astype(jnp.float32).T, upstream[inner_step].astype(jnp.float32), preferred_element_type=jnp.float32) * factor
            first_state = BETA_FIRST * first_state + (1.0 - BETA_FIRST) * gradient
            second = BETA_SECOND * second + (1.0 - BETA_SECOND) * gradient * gradient
            weights = weights - INNER_RATE * (first_state / (jnp.sqrt(second) + EPSILON) + WEIGHT_DECAY * weights)
        mixed = MIXING * weights + (1.0 - MIXING) * global_new
        return (mixed, first_state, jnp.stack(results))
    merged, new_first_moment, input_grad = lax.map(worker, (activations, cotangent, params, first_moment, second_moment))
    return (merged, new_first_moment, input_grad)
```

```python
import jax
import jax.numpy as jnp
from jax import lax
from jax.experimental import pallas as pl
from jax.experimental.pallas import tpu as pltpu
from jax.sharding import PartitionSpec as P

D = 4096
KVW = 512
ROWS = 256
TOKENS = 128
RING = 4
LINE = 4
SPAN = ROWS * LINE
HALF = ROWS // 2
CHIPS = 8
CHUNK = ROWS // CHIPS
REPLICAS = 32

BETA_FIRST = 0.9
BETA_SECOND = 0.95
EPSILON = 1e-08
WEIGHT_DECAY = 0.1
INNER_RATE = 0.03
OUTER_RATE = 0.7
OUTER_MOMENT = 0.9
MIXING = 0.5

FACTOR = float(D) ** (-0.5)
MESH = pl.DeviceIdType.MESH
BF16 = jnp.bfloat16
F32 = jnp.float32


def kernel(
    act,
    cot,
    params,
    first,
    second,
    anchor,
    outer,
    merged_out,
    first_out,
    grad_out,
    acts,
    cots,
    scaled,
    partial,
    landed,
    relay,
    back,
    weights,
    firsts,
    seconds,
    anchors,
    outers,
    rounded,
    got_a,
    sum_a,
    sent_b,
    got_b,
    total,
    local_sem,
    cot_s,
    cot_r,
    act_s,
    act_r,
    w_s,
    w_r,
    part_s,
    part_r,
    back_s,
    back_r,
    a_s,
    a_r,
    b_s,
    b_r,
    d_s,
    d_r,
    out_sem,
):
    replica = lax.axis_index("replica")
    shard = lax.axis_index("fsdp")
    y, p = shard // LINE, shard % LINE
    group, m = replica // CHIPS, replica % CHIPS
    edge = (p == 0) | (p == LINE - 1)
    inner = (p == 1) | (p == 2)
    has_low, has_high = p > 0, p < LINE - 1
    upper = p // 2

    def mirrored(at):
        return at + upper * (LINE - 1 - 2 * at)

    is_end = 1 - (p + 1) % LINE // 2
    order = [mirrored(3), mirrored(2), mirrored(is_end), p]
    near = [p, mirrored(is_end), mirrored(2), mirrored(3)]
    ring = [lax.rem(y + j, RING) for j in range(RING)]
    chip = [lax.rem(m + j, CHIPS) for j in range(CHIPS)]
    swaps = [group + 1 - 2 * (group % 2), 3 - group]

    def on_ring(j):
        return {"fsdp": ring[j] * LINE + p}

    def on_line(at):
        return {"fsdp": y * LINE + at}

    def on_chip(j):
        return {"replica": group * CHIPS + chip[j]}

    def on_group(step):
        return {"replica": swaps[step] * CHIPS + m}

    def remote(src, dst, send, recv, where):
        return pltpu.make_async_remote_copy(
            src_ref=src,
            dst_ref=dst,
            send_sem=send,
            recv_sem=recv,
            device_id=where,
            device_id_type=MESH,
        )

    def rows_of(at, size):
        return pl.ds(pl.multiple_of(at * size, size), size)

    def features(ring_at, line_at):
        return pl.ds(pl.multiple_of(ring_at * SPAN + line_at * ROWS, ROWS), ROWS)

    own_rows = rows_of(y, TOKENS)
    loads = [
        pltpu.make_async_copy(params, weights, local_sem.at[0]),
        pltpu.make_async_copy(cot, cots.at[own_rows], local_sem.at[1]),
    ]
    for k in range(LINE):
        loads.append(
            pltpu.make_async_copy(
                act.at[:, features(y, order[k])], acts.at[k, own_rows], local_sem.at[2 + k]
            )
        )
    loads += [
        pltpu.make_async_copy(anchor, anchors, local_sem.at[6]),
        pltpu.make_async_copy(outer, outers, local_sem.at[7]),
        pltpu.make_async_copy(first, firsts, local_sem.at[8]),
        pltpu.make_async_copy(second, seconds, local_sem.at[9]),
    ]
    for load in loads:
        load.start()

    barrier = pltpu.get_barrier_semaphore()

    def greet(where):
        pl.semaphore_signal(barrier, inc=1, device_id=where, device_id_type=MESH)

    for step in range(2):
        greet(on_group(step))
    for j in range(1, CHIPS):
        greet(on_chip(j))
    for j in range(1, RING):
        greet(on_ring(j))

    @pl.when(has_low)
    def _():
        greet(on_line(p - 1))

    @pl.when(has_high)
    def _():
        greet(on_line(p + 1))

    with jax.named_scope("scale"):
        loads[0].wait()
        scaled[p] = (weights[...] * FACTOR).astype(BF16)
        rounded[...] = weights[...].astype(BF16)

    with jax.named_scope("barrier"):
        met = 2 + (CHIPS - 1) + (RING - 1)
        pl.semaphore_wait(barrier, met + 2 - is_end)

    cot_copies = [
        remote(cot, cots.at[own_rows], cot_s.at[j], cot_r.at[j], on_ring(j))
        for j in range(1, RING)
    ]
    act_copies = [
        [
            remote(
                act.at[:, features(ring[j], order[k])],
                acts.at[k, own_rows],
                act_s.at[k, j],
                act_r.at[k, j],
                on_ring(j),
            )
            for j in range(1, RING)
        ]
        for k in range(LINE)
    ]
    a_copies = [
        remote(
            rounded.at[rows_of(chip[j], CHUNK)],
            got_a.at[j],
            a_s.at[j],
            a_r.at[j],
            on_chip(j),
        )
        for j in range(1, CHIPS)
    ]
    b_copies = [
        remote(sent_b.at[step], got_b.at[step], b_s.at[step], b_r.at[step], on_group(step))
        for step in range(2)
    ]
    d_copies = [
        remote(total.at[m], total.at[m], d_s.at[j], d_r.at[j], on_chip(j))
        for j in range(1, CHIPS)
    ]

    def d_arrival(j):
        origin = lax.rem(m - j + CHIPS, CHIPS)
        return remote(total.at[origin], total.at[origin], d_s.at[j], d_r.at[j], on_chip(j))

    def w_copy(block, half, way, to):
        rows = scaled.at[block, pl.ds(half * HALF, HALF)]
        return remote(rows, rows, w_s.at[way, block, half], w_r.at[block, half], on_line(to))

    def part_copy(k, half, way, to):
        rows = pl.ds(half * HALF, HALF)
        return remote(
            relay.at[k, rows],
            landed.at[way, order[k], rows],
            part_s.at[k, half],
            part_r.at[way, order[k], half],
            on_line(to),
        )

    def part_arrival(way, block, half):
        rows = landed.at[way, block, pl.ds(half * HALF, HALF)]
        return remote(rows, rows, part_s.at[0, half], part_r.at[way, block, half], on_line(p))

    def back_copy(i, j):
        return remote(
            back.at[i, rows_of(ring[j], TOKENS)],
            grad_out.at[:, features(y, near[i])],
            back_s.at[i, j],
            back_r.at[i, j],
            on_ring(j),
        )

    def back_own(i):
        return pltpu.make_async_copy(
            back.at[i, own_rows], grad_out.at[:, features(y, near[i])], out_sem.at[i]
        )

    for copy in a_copies + cot_copies:
        copy.start()
    for half in range(2):

        @pl.when(has_low)
        def _():
            w_copy(p, half, 1, p - 1).start()

        @pl.when(has_high)
        def _():
            w_copy(p, half, 0, p + 1).start()

    for copies in act_copies:
        for copy in copies:
            copy.start()

    def pass_near(half):
        @pl.when(inner)
        def _():
            w_copy(p - 1, half, 0, p + 1).wait_recv()
            w_copy(p - 1, half, 0, p + 1).start()
            w_copy(p + 1, half, 1, p - 1).wait_recv()
            w_copy(p + 1, half, 1, p - 1).start()

    def pass_far(half):
        @pl.when(p == 1)
        def _():
            w_copy(3, half, 1, 0).wait_recv()
            w_copy(3, half, 1, 0).start()

        @pl.when(p == 2)
        def _():
            w_copy(0, half, 0, 3).wait_recv()
            w_copy(0, half, 0, 3).start()

    def at_end_wait(block):
        @pl.when(edge)
        def _():
            for half in range(2):
                w_copy(block, half, 0, p).wait_recv()

    def input_grad(i):
        back[i] = lax.dot_general(
            cots[...],
            scaled[near[i]],
            (((1,), (1,)), ((), ())),
            preferred_element_type=F32,
        ).astype(BF16)
        for j in range(1, RING):
            back_copy(i, j).start()
        back_own(i).start()

    def gradient(k):
        for copy in act_copies[k]:
            copy.wait_recv()
        loads[2 + k].wait()
        with jax.named_scope("product"):
            partial[k] = lax.dot_general(
                acts[k], cots[...], (((0,), (0,)), ((), ())), preferred_element_type=F32
            )
        if k == LINE - 1:
            return

        @pl.when(edge)
        def _():
            relay[k] = partial[k].astype(BF16)

        @pl.when(p == 0)
        def _():
            for half in range(2):
                part_copy(k, half, 0, 1).start()

        @pl.when(p == LINE - 1)
        def _():
            for half in range(2):
                part_copy(k, half, 1, LINE - 2).start()

    def pass_part(k, half):
        rows = pl.ds(half * HALF, HALF)

        @pl.when(inner)
        def _():
            goes_up = order[k] > p

            @pl.when(goes_up)
            def _():
                part_arrival(0, order[k], half).wait_recv()
                both = partial[k, rows] + landed[0, order[k], rows].astype(F32)
                relay[k, rows] = both.astype(BF16)
                part_copy(k, half, 0, p + 1).start()

            @pl.when(order[k] < p)
            def _():
                part_arrival(1, order[k], half).wait_recv()
                both = partial[k, rows] + landed[1, order[k], rows].astype(F32)
                relay[k, rows] = both.astype(BF16)
                part_copy(k, half, 1, p - 1).start()

    with jax.named_scope("pass_near0"):
        pass_near(0)
    with jax.named_scope("sum_a"):
        own_sum = weights[rows_of(m, CHUNK)]
        for j in range(1, CHIPS):
            a_copies[j - 1].wait_recv()
            own_sum += got_a[j].astype(F32)
        sum_a[...] = own_sum
        sent_b[0] = own_sum.astype(BF16)
        b_copies[0].start()
    with jax.named_scope("pass_near1"):
        pass_near(1)
    with jax.named_scope("cot"):
        loads[1].wait()
        for copy in cot_copies:
            copy.wait_recv()
    with jax.named_scope("ig0"):
        input_grad(0)
    with jax.named_scope("pass_far0"):
        pass_far(0)
    with jax.named_scope("grad0"):
        gradient(0)
    with jax.named_scope("sum_b0"):
        b_copies[0].wait_recv()
        sum_a[...] += got_b[0].astype(F32)
        sent_b[1] = sum_a[...].astype(BF16)
        b_copies[1].start()
    with jax.named_scope("pass_far1"):
        pass_far(1)
    with jax.named_scope("grad1"):
        gradient(1)
    with jax.named_scope("ig1"):
        at_end_wait(near[1])
        input_grad(1)
    with jax.named_scope("part0"):
        pass_part(0, 0)
        pass_part(0, 1)
    with jax.named_scope("grad2"):
        gradient(2)
    with jax.named_scope("sum_b1"):
        b_copies[1].wait_recv()
        sum_a[...] += got_b[1].astype(F32)
        total[m] = sum_a[...].astype(BF16)
        for copy in d_copies:
            copy.start()
    with jax.named_scope("ig2"):
        at_end_wait(near[2])
        input_grad(2)
    with jax.named_scope("grad3"):
        gradient(3)
    with jax.named_scope("part1"):
        pass_part(1, 0)
        pass_part(1, 1)
    with jax.named_scope("ig3"):
        at_end_wait(near[3])
        input_grad(3)
    with jax.named_scope("part2"):
        pass_part(2, 0)
        pass_part(2, 1)
    with jax.named_scope("outer"):
        for j in range(1, CHIPS):
            d_arrival(j).wait_recv()
        for load in loads[6:]:
            load.wait()
        mean = total[...].astype(F32).reshape(ROWS, KVW) * (1.0 / REPLICAS)
        old = anchors[...].astype(F32)
        outer_grad = old - mean
        moment = OUTER_MOMENT * outers[...].astype(F32) + outer_grad
        new = old - OUTER_RATE * (outer_grad + OUTER_MOMENT * moment)
        kept = MIXING * (1.0 - INNER_RATE * WEIGHT_DECAY)
        partial[0] = kept * weights[...] + (1.0 - MIXING) * new

    stores = []
    for half in range(2):
        rows = pl.ds(half * HALF, HALF)
        with jax.named_scope("last%d" % half):

            @pl.when(has_low)
            def _():
                part_arrival(0, p, half).wait_recv()
                partial[3, rows] += landed[0, p, rows].astype(F32)

            @pl.when(has_high)
            def _():
                part_arrival(1, p, half).wait_recv()
                partial[3, rows] += landed[1, p, rows].astype(F32)

            gradient_now = partial[3, rows] * FACTOR
            moment = BETA_FIRST * firsts[rows].astype(F32) + (1.0 - BETA_FIRST) * gradient_now
            spread = (
                BETA_SECOND * seconds[rows] + (1.0 - BETA_SECOND) * gradient_now * gradient_now
            )
            step = moment / (jnp.sqrt(spread) + EPSILON)
            partial[1, rows] = moment
            partial[2, rows] = partial[0, rows] - (MIXING * INNER_RATE) * step
            for slot, out in ((1, first_out), (2, merged_out)):
                store = pltpu.make_async_copy(
                    partial.at[slot, rows], out.at[rows], out_sem.at[LINE + 2 * half + slot - 1]
                )
                store.start()
                stores.append(store)

    with jax.named_scope("drain_back"):
        for i in range(LINE):
            for j in range(1, RING):
                back_copy(i, j).wait_recv()
    with jax.named_scope("drain"):
        for i in range(LINE):
            back_own(i).wait()
            for j in range(1, RING):
                back_copy(i, j).wait_send()
        for store in stores:
            store.wait()
        for copy in cot_copies + a_copies + b_copies + d_copies:
            copy.wait_send()
        for copies in act_copies:
            for copy in copies:
                copy.wait_send()
        for half in range(2):

            @pl.when(has_low)
            def _():
                w_copy(p, half, 1, p - 1).wait_send()

            @pl.when(has_high)
            def _():
                w_copy(p, half, 0, p + 1).wait_send()

            @pl.when(inner)
            def _():
                w_copy(p - 1, half, 0, p + 1).wait_send()
                w_copy(p + 1, half, 1, p - 1).wait_send()

            @pl.when(p == 1)
            def _():
                w_copy(3, half, 1, 0).wait_send()

            @pl.when(p == 2)
            def _():
                w_copy(0, half, 0, 3).wait_send()

            for k in range(LINE - 1):
                part_copy(k, half, 0, p).wait_send()


def on_device(activations, cotangent, params, first_moment, second_moment, anchor, outer_momentum):
    any_spec = pl.BlockSpec(memory_space=pl.ANY)
    dma = pltpu.SemaphoreType.DMA
    merged, first, grad = pl.pallas_call(
        kernel,
        out_shape=(
            jax.ShapeDtypeStruct((ROWS, KVW), F32),
            jax.ShapeDtypeStruct((ROWS, KVW), F32),
            jax.ShapeDtypeStruct((TOKENS, D), BF16),
        ),
        in_specs=[any_spec] * 7,
        out_specs=(any_spec,) * 3,
        scratch_shapes=[
            pltpu.VMEM((LINE, RING * TOKENS, ROWS), BF16),
            pltpu.VMEM((RING * TOKENS, KVW), BF16),
            pltpu.VMEM((LINE, ROWS, KVW), BF16),
            pltpu.VMEM((LINE, ROWS, KVW), F32),
            pltpu.VMEM((2, LINE, ROWS, KVW), BF16),
            pltpu.VMEM((LINE - 1, ROWS, KVW), BF16),
            pltpu.VMEM((LINE, RING * TOKENS, ROWS), BF16),
            pltpu.VMEM((ROWS, KVW), F32),
            pltpu.VMEM((ROWS, KVW), BF16),
            pltpu.VMEM((ROWS, KVW), F32),
            pltpu.VMEM((ROWS, KVW), BF16),
            pltpu.VMEM((ROWS, KVW), BF16),
            pltpu.VMEM((ROWS, KVW), BF16),
            pltpu.VMEM((CHIPS, CHUNK, KVW), BF16),
            pltpu.VMEM((CHUNK, KVW), F32),
            pltpu.VMEM((2, CHUNK, KVW), BF16),
            pltpu.VMEM((2, CHUNK, KVW), BF16),
            pltpu.VMEM((CHIPS, CHUNK, KVW), BF16),
            dma((10,)),
            dma((RING,)),
            dma((RING,)),
            dma((LINE, RING)),
            dma((LINE, RING)),
            dma((2, LINE, 2)),
            dma((LINE, 2)),
            dma((LINE - 1, 2)),
            dma((2, LINE, 2)),
            dma((LINE, RING)),
            dma((LINE, RING)),
            dma((CHIPS,)),
            dma((CHIPS,)),
            dma((2,)),
            dma((2,)),
            dma((CHIPS,)),
            dma((CHIPS,)),
            dma((2 * LINE,)),
        ],
        compiler_params=pltpu.CompilerParams(
            collective_id=0, has_side_effects=True, vmem_limit_bytes=56 * 2**20
        ),
        name="diloco_step",
    )(
        activations[0, 0],
        cotangent[0, 0],
        params[0],
        first_moment[0],
        second_moment[0],
        anchor,
        outer_momentum,
    )
    return merged[None], first[None], grad[None, None]


def solution(mesh):
    placed = (
        P("replica", None, "fsdp", None),
        P("replica", None, "fsdp", None),
        P("replica", "fsdp", None),
        P("replica", "fsdp", None),
        P("replica", "fsdp", None),
        P("fsdp", None),
        P("fsdp", None),
    )
    return jax.shard_map(
        on_device,
        mesh=mesh,
        in_specs=placed,
        out_specs=(
            P("replica", "fsdp", None),
            P("replica", "fsdp", None),
            P("replica", None, "fsdp", None),
        ),
        check_vma=False,
    )
```

```python
import jax
import jax.numpy as jnp
from jax import lax
from jax.experimental import pallas as pl
from jax.experimental.pallas import tpu as pltpu
from jax.sharding import PartitionSpec as P

D = 4096
KVW = 512
ROWS = 256
TOKENS = 128
RING = 4
LINE = 4
SPAN = ROWS * LINE
HALF = ROWS // 2
WIDE = KVW // 2
CHIPS = 8
CHUNK = ROWS // CHIPS
REPLICAS = 32

BETA_FIRST = 0.9
BETA_SECOND = 0.95
EPSILON = 1e-08
WEIGHT_DECAY = 0.1
INNER_RATE = 0.03
OUTER_RATE = 0.7
OUTER_MOMENT = 0.9
MIXING = 0.5

FACTOR = float(D) ** (-0.5)
MESH = pl.DeviceIdType.MESH
BF16 = jnp.bfloat16
F32 = jnp.float32


def kernel(
    act,
    cot,
    params,
    first,
    second,
    anchor,
    outer,
    merged_out,
    first_out,
    grad_out,
    acts,
    cots,
    scaled,
    partial,
    landed,
    relay,
    back,
    weights,
    firsts,
    seconds,
    anchors,
    outers,
    mixed,
    rounded,
    got_a,
    sum_a,
    sent_b,
    got_b,
    total,
    near_sem,
    far_sem,
    local_sem,
    cot_s,
    cot_r,
    act_s,
    act_r,
    w_s,
    w_r,
    part_s,
    part_r,
    back_s,
    back_r,
    a_s,
    a_r,
    b_s,
    b_r,
    d_s,
    d_r,
    out_sem,
):
    replica = lax.axis_index("replica")
    shard = lax.axis_index("fsdp")
    y, p = shard // LINE, shard % LINE
    group, m = replica // CHIPS, replica % CHIPS
    core = replica % 2
    edge = (p == 0) | (p == LINE - 1)
    inner = (p == 1) | (p == 2)
    has_low, has_high = p > 0, p < LINE - 1
    upper = p // 2

    def mirrored(at):
        return at + upper * (LINE - 1 - 2 * at)

    is_end = 1 - (p + 1) % LINE // 2
    order = [mirrored(3), mirrored(2), mirrored(is_end), p]
    near = [p, mirrored(is_end), mirrored(2), mirrored(3)]
    ring = [lax.rem(y + j, RING) for j in range(RING)]
    chip = [lax.rem(m + j, CHIPS) for j in range(CHIPS)]
    swaps = [group + 1 - 2 * (group % 2), 3 - group]

    def on_ring(j):
        return {"fsdp": ring[j] * LINE + p}

    def on_line(at):
        return {"fsdp": y * LINE + at}

    def on_chip(j):
        return {"replica": group * CHIPS + chip[j]}

    def on_group(step):
        return {"replica": swaps[step] * CHIPS + m}

    def remote(src, dst, send, recv, where):
        return pltpu.make_async_remote_copy(
            src_ref=src,
            dst_ref=dst,
            send_sem=send,
            recv_sem=recv,
            device_id=where,
            device_id_type=MESH,
        )

    def rows_of(at, size):
        return pl.ds(pl.multiple_of(at * size, size), size)

    def features(ring_at, line_at):
        return pl.ds(pl.multiple_of(ring_at * SPAN + line_at * ROWS, ROWS), ROWS)

    def columns(half):
        return pl.ds(half * WIDE, WIDE)

    barrier = pltpu.get_barrier_semaphore()

    def signal(semaphore, where):
        pl.semaphore_signal(semaphore, inc=1, device_id=where, device_id_type=MESH)

    gate = replica - core
    for j in range(1, RING):
        signal(barrier, {"replica": gate, "fsdp": ring[j] * LINE + p})

    @pl.when(has_low)
    def _():
        signal(barrier, {"replica": gate, "fsdp": shard - 1})

    @pl.when(has_high)
    def _():
        signal(barrier, {"replica": gate, "fsdp": shard + 1})

    for j in range(2, CHIPS, 2):
        signal(barrier, {"replica": group * CHIPS + lax.rem(m - core + j, CHIPS)})

    @pl.when(core == 1)
    def _():
        signal(barrier, {"replica": gate})

    own_rows = rows_of(y, TOKENS)
    loads = [
        pltpu.make_async_copy(params, weights, local_sem.at[0]),
        pltpu.make_async_copy(cot, cots.at[own_rows], local_sem.at[1]),
    ]
    for k in range(LINE):
        loads.append(
            pltpu.make_async_copy(
                act.at[:, features(y, order[k])], acts.at[k, own_rows], local_sem.at[2 + k]
            )
        )
    loads += [
        pltpu.make_async_copy(anchor, anchors, local_sem.at[6]),
        pltpu.make_async_copy(outer, outers, local_sem.at[7]),
        pltpu.make_async_copy(first, firsts, local_sem.at[8]),
        pltpu.make_async_copy(second, seconds, local_sem.at[9]),
    ]
    for load in loads:
        load.start()

    with jax.named_scope("scale"):
        loads[0].wait()
        scaled[p] = (weights[...] * FACTOR).astype(BF16)
        rounded[...] = weights[...].astype(BF16)

    with jax.named_scope("gate"):

        @pl.when(core == 0)
        def _():
            pl.semaphore_wait(barrier, 2 * (RING - 1) + (CHIPS - 2) + 1 + 2 * (2 - is_end))
            signal(near_sem, {"replica": gate + 1})

        @pl.when(core == 1)
        def _():
            pl.semaphore_wait(near_sem, 1)
            for step in range(2):
                signal(barrier, on_group(step))

    def await_far():
        @pl.when(core == 1)
        def _():
            pl.semaphore_wait(barrier, 2)
            signal(far_sem, {"replica": gate})

        @pl.when(core == 0)
        def _():
            pl.semaphore_wait(far_sem, 1)

    cot_copies = [
        [
            remote(
                cot.at[:, columns(half)],
                cots.at[own_rows, columns(half)],
                cot_s.at[half, j],
                cot_r.at[half, j],
                on_ring(j),
            )
            for j in range(1, RING)
        ]
        for half in range(2)
    ]
    act_copies = [
        [
            remote(
                act.at[:, features(ring[j], order[k])],
                acts.at[k, own_rows],
                act_s.at[k, j],
                act_r.at[k, j],
                on_ring(j),
            )
            for j in range(1, RING)
        ]
        for k in range(LINE)
    ]
    a_copies = [
        remote(
            rounded.at[rows_of(chip[j], CHUNK)],
            got_a.at[j],
            a_s.at[j],
            a_r.at[j],
            on_chip(j),
        )
        for j in range(1, CHIPS)
    ]
    b_copies = [
        remote(sent_b.at[step], got_b.at[step], b_s.at[step], b_r.at[step], on_group(step))
        for step in range(2)
    ]
    d_copies = [
        remote(total.at[m], total.at[m], d_s.at[j], d_r.at[j], on_chip(j))
        for j in range(1, CHIPS)
    ]

    def d_arrival(j):
        origin = lax.rem(m - j + CHIPS, CHIPS)
        return remote(total.at[origin], total.at[origin], d_s.at[j], d_r.at[j], on_chip(j))

    def w_copy(block, half, way, to):
        rows = scaled.at[block, pl.ds(half * HALF, HALF)]
        return remote(rows, rows, w_s.at[way, block, half], w_r.at[block, half], on_line(to))

    def part_copy(k, half, way, to):
        return remote(
            relay.at[k, half],
            landed.at[way, order[k], half],
            part_s.at[k, half],
            part_r.at[way, order[k], half],
            on_line(to),
        )

    def part_arrival(way, block, half):
        piece = landed.at[way, block, half]
        return remote(piece, piece, part_s.at[0, half], part_r.at[way, block, half], on_line(p))

    def back_copy(i, j):
        return remote(
            back.at[i, rows_of(ring[j], TOKENS)],
            grad_out.at[:, features(y, near[i])],
            back_s.at[i, j],
            back_r.at[i, j],
            on_ring(j),
        )

    def back_own(i):
        return pltpu.make_async_copy(
            back.at[i, own_rows], grad_out.at[:, features(y, near[i])], out_sem.at[i]
        )

    for half in range(2):

        @pl.when(has_low)
        def _():
            w_copy(p, half, 1, p - 1).start()

        @pl.when(has_high)
        def _():
            w_copy(p, half, 0, p + 1).start()

    in_turn = [cot_copies[0], act_copies[0], cot_copies[1], a_copies] + act_copies[1:]
    for copies in in_turn:
        for copy in copies:
            copy.start()

    def pass_near(half):
        @pl.when(inner)
        def _():
            w_copy(p - 1, half, 0, p + 1).wait_recv()
            w_copy(p - 1, half, 0, p + 1).start()
            w_copy(p + 1, half, 1, p - 1).wait_recv()
            w_copy(p + 1, half, 1, p - 1).start()

    def pass_far(half):
        @pl.when(p == 1)
        def _():
            w_copy(3, half, 1, 0).wait_recv()
            w_copy(3, half, 1, 0).start()

        @pl.when(p == 2)
        def _():
            w_copy(0, half, 0, 3).wait_recv()
            w_copy(0, half, 0, 3).start()

    def at_end_wait(block):
        @pl.when(edge)
        def _():
            for half in range(2):
                w_copy(block, half, 0, p).wait_recv()

    def input_grad(i):
        with jax.named_scope("ig%d" % i):
            if i > 0:
                at_end_wait(near[i])
            back[i] = lax.dot_general(
                cots[...],
                scaled[near[i]],
                (((1,), (1,)), ((), ())),
                preferred_element_type=F32,
            ).astype(BF16)
            for j in range(1, RING):
                back_copy(i, j).start()
            back_own(i).start()

    def product(k, half):
        partial[k, :, columns(half)] = lax.dot_general(
            acts[k],
            cots[:, columns(half)],
            (((0,), (0,)), ((), ())),
            preferred_element_type=F32,
        )
        if k == LINE - 1:
            return

        @pl.when(edge)
        def _():
            relay[k, half] = partial[k, :, columns(half)].astype(BF16)

        @pl.when(p == 0)
        def _():
            part_copy(k, half, 0, 1).start()

        @pl.when(p == LINE - 1)
        def _():
            part_copy(k, half, 1, LINE - 2).start()

    def act_wait(k):
        for copy in act_copies[k]:
            copy.wait_recv()
        loads[2 + k].wait()

    def gradient(k):
        with jax.named_scope("grad%d" % k):
            act_wait(k)
            product(k, 0)
            product(k, 1)

    def pass_part(k, half):
        def onward(way, to):
            part_arrival(way, order[k], half).wait_recv()
            both = partial[k, :, columns(half)] + landed[way, order[k], half].astype(F32)
            relay[k, half] = both.astype(BF16)
            part_copy(k, half, way, to).start()

        with jax.named_scope("part%d%d" % (k, half)):

            @pl.when(inner & (order[k] > p))
            def _():
                onward(0, p + 1)

            @pl.when(inner & (order[k] < p))
            def _():
                onward(1, p - 1)

    def outer_step(step):
        if step == 0:
            await_far()
            b_copies[0].start()
            return
        b_copies[step - 1].wait_recv()
        sum_a[...] += got_b[step - 1].astype(F32)
        if step == 1:
            sent_b[1] = sum_a[...].astype(BF16)
            b_copies[1].start()
            return
        total[m] = sum_a[...].astype(BF16)
        for copy in d_copies:
            copy.start()

    def outer_turn(turn):
        with jax.named_scope("outer_turn%d" % turn):
            if turn < 3:

                @pl.when(group > 0)
                def _():
                    outer_step(turn)

            if turn > 0:

                @pl.when(group == 0)
                def _():
                    outer_step(turn - 1)

    with jax.named_scope("pass_near0"):
        pass_near(0)
    with jax.named_scope("sum_a"):
        own_sum = weights[rows_of(m, CHUNK)]
        for j in range(1, CHIPS):
            a_copies[j - 1].wait_recv()
            own_sum += got_a[j].astype(F32)
        sum_a[...] = own_sum
        sent_b[0] = own_sum.astype(BF16)
    with jax.named_scope("pass_near1"):
        pass_near(1)
    outer_turn(0)
    with jax.named_scope("grad00"):
        loads[1].wait()
        for copy in cot_copies[0]:
            copy.wait_recv()
        act_wait(0)
        product(0, 0)
    with jax.named_scope("grad01"):
        for copy in cot_copies[1]:
            copy.wait_recv()
        product(0, 1)
    with jax.named_scope("pass_far0"):
        pass_far(0)
    outer_turn(1)
    input_grad(0)
    with jax.named_scope("pass_far1"):
        pass_far(1)
    pass_part(0, 0)
    gradient(1)
    input_grad(1)
    pass_part(0, 1)
    gradient(2)
    outer_turn(2)
    input_grad(2)
    pass_part(2, 0)
    pass_part(1, 0)
    gradient(3)
    pass_part(2, 1)
    input_grad(3)
    pass_part(1, 1)
    outer_turn(3)
    with jax.named_scope("outer"):
        for load in loads[6:]:
            load.wait()
        for j in range(1, CHIPS):
            d_arrival(j).wait_recv()
        mean = total[...].astype(F32).reshape(ROWS, KVW) * (1.0 / REPLICAS)
        old = anchors[...].astype(F32)
        outer_grad = old - mean
        moment = OUTER_MOMENT * outers[...].astype(F32) + outer_grad
        new = old - OUTER_RATE * (outer_grad + OUTER_MOMENT * moment)
        kept = MIXING * (1.0 - INNER_RATE * WEIGHT_DECAY)
        mixed[...] = kept * weights[...] + (1.0 - MIXING) * new

    for half in range(2):
        cut = columns(half)
        with jax.named_scope("last%d" % half):

            @pl.when(has_low)
            def _():
                part_arrival(0, p, half).wait_recv()
                partial[3, :, cut] += landed[0, p, half].astype(F32)

            @pl.when(has_high)
            def _():
                part_arrival(1, p, half).wait_recv()
                partial[3, :, cut] += landed[1, p, half].astype(F32)

            gradient_now = partial[3, :, cut] * FACTOR
            moment = BETA_FIRST * firsts[:, cut].astype(F32) + (1.0 - BETA_FIRST) * gradient_now
            spread = (
                BETA_SECOND * seconds[:, cut] + (1.0 - BETA_SECOND) * gradient_now * gradient_now
            )
            step = moment / (jnp.sqrt(spread) + EPSILON)
            first_out[:, cut] = moment
            merged_out[:, cut] = mixed[:, cut] - (MIXING * INNER_RATE) * step

    with jax.named_scope("drain_back"):
        for i in range(LINE):
            for j in range(1, RING):
                back_copy(i, j).wait_recv()
    with jax.named_scope("drain"):
        for i in range(LINE):
            back_own(i).wait()
            for j in range(1, RING):
                back_copy(i, j).wait_send()
        for copies in in_turn + [b_copies, d_copies]:
            for copy in copies:
                copy.wait_send()
        for half in range(2):

            @pl.when(has_low)
            def _():
                w_copy(p, half, 1, p - 1).wait_send()

            @pl.when(has_high)
            def _():
                w_copy(p, half, 0, p + 1).wait_send()

            @pl.when(inner)
            def _():
                w_copy(p - 1, half, 0, p + 1).wait_send()
                w_copy(p + 1, half, 1, p - 1).wait_send()

            @pl.when(p == 1)
            def _():
                w_copy(3, half, 1, 0).wait_send()

            @pl.when(p == 2)
            def _():
                w_copy(0, half, 0, 3).wait_send()

            for k in range(LINE - 1):
                part_copy(k, half, 0, p).wait_send()


def write_out(merged, first, grad, merged_out, first_out, grad_out, sem):
    copies = [
        pltpu.make_async_copy(merged, merged_out, sem.at[0]),
        pltpu.make_async_copy(first, first_out, sem.at[1]),
        pltpu.make_async_copy(grad, grad_out, sem.at[2]),
    ]
    for copy in copies:
        copy.start()
    for copy in copies:
        copy.wait()


def on_device(activations, cotangent, params, first_moment, second_moment, anchor, outer_momentum):
    any_spec = pl.BlockSpec(memory_space=pl.ANY)
    vmem_spec = pl.BlockSpec(memory_space=pltpu.VMEM)
    dma = pltpu.SemaphoreType.DMA
    results = (
        jax.ShapeDtypeStruct((ROWS, KVW), F32),
        jax.ShapeDtypeStruct((ROWS, KVW), F32),
        jax.ShapeDtypeStruct((TOKENS, D), BF16),
    )
    held = pl.pallas_call(
        kernel,
        out_shape=tuple(pltpu.VMEM(r.shape, r.dtype) for r in results),
        in_specs=[any_spec] * 7,
        out_specs=(vmem_spec,) * 3,
        scratch_shapes=[
            pltpu.VMEM((LINE, RING * TOKENS, ROWS), BF16),
            pltpu.VMEM((RING * TOKENS, KVW), BF16),
            pltpu.VMEM((LINE, ROWS, KVW), BF16),
            pltpu.VMEM((LINE, ROWS, KVW), F32),
            pltpu.VMEM((2, LINE, 2, ROWS, WIDE), BF16),
            pltpu.VMEM((LINE - 1, 2, ROWS, WIDE), BF16),
            pltpu.VMEM((LINE, RING * TOKENS, ROWS), BF16),
            pltpu.VMEM((ROWS, KVW), F32),
            pltpu.VMEM((ROWS, KVW), BF16),
            pltpu.VMEM((ROWS, KVW), F32),
            pltpu.VMEM((ROWS, KVW), BF16),
            pltpu.VMEM((ROWS, KVW), BF16),
            pltpu.VMEM((ROWS, KVW), F32),
            pltpu.VMEM((ROWS, KVW), BF16),
            pltpu.VMEM((CHIPS, CHUNK, KVW), BF16),
            pltpu.VMEM((CHUNK, KVW), F32),
            pltpu.VMEM((2, CHUNK, KVW), BF16),
            pltpu.VMEM((2, CHUNK, KVW), BF16),
            pltpu.VMEM((CHIPS, CHUNK, KVW), BF16),
            pltpu.SemaphoreType.REGULAR,
            pltpu.SemaphoreType.REGULAR,
            dma((10,)),
            dma((2, RING)),
            dma((2, RING)),
            dma((LINE, RING)),
            dma((LINE, RING)),
            dma((2, LINE, 2)),
            dma((LINE, 2)),
            dma((LINE - 1, 2)),
            dma((2, LINE, 2)),
            dma((LINE, RING)),
            dma((LINE, RING)),
            dma((CHIPS,)),
            dma((CHIPS,)),
            dma((2,)),
            dma((2,)),
            dma((CHIPS,)),
            dma((CHIPS,)),
            dma((LINE,)),
        ],
        compiler_params=pltpu.CompilerParams(
            collective_id=0, has_side_effects=True, vmem_limit_bytes=58 * 2**20
        ),
        name="diloco_step",
    )(
        activations[0, 0],
        cotangent[0, 0],
        params[0],
        first_moment[0],
        second_moment[0],
        anchor,
        outer_momentum,
    )
    merged, first, grad = pl.pallas_call(
        write_out,
        out_shape=results,
        in_specs=[vmem_spec] * 3,
        out_specs=(any_spec,) * 3,
        scratch_shapes=[dma((3,))],
        name="write_out",
    )(*(pltpu.with_memory_space_constraint(x, pltpu.VMEM) for x in held))
    return merged[None], first[None], grad[None, None]


def solution(mesh):
    placed = (
        P("replica", None, "fsdp", None),
        P("replica", None, "fsdp", None),
        P("replica", "fsdp", None),
        P("replica", "fsdp", None),
        P("replica", "fsdp", None),
        P("fsdp", None),
        P("fsdp", None),
    )
    return jax.shard_map(
        on_device,
        mesh=mesh,
        in_specs=placed,
        out_specs=(
            P("replica", "fsdp", None),
            P("replica", "fsdp", None),
            P("replica", None, "fsdp", None),
        ),
        check_vma=False,
    )
```

```python
import jax
import jax.numpy as jnp
from jax import lax
from jax.experimental import pallas as pl
from jax.experimental.pallas import tpu as pltpu
from jax.sharding import PartitionSpec as P

D = 4096
KVW = 512
ROWS = 256
TOKENS = 128
RING = 4
LINE = 4
GROUPS = 4
SPAN = ROWS * LINE
HALF = ROWS // 2
WIDE = KVW // 2
CHIPS = 8
CHUNK = ROWS // CHIPS
REPLICAS = 32

BETA_FIRST = 0.9
BETA_SECOND = 0.95
EPSILON = 1e-08
WEIGHT_DECAY = 0.1
INNER_RATE = 0.03
OUTER_RATE = 0.7
OUTER_MOMENT = 0.9
MIXING = 0.5

FACTOR = float(D) ** (-0.5)
SWAPS_AT = (
    ((2, 0), (3, 0)),
    ((1, 0),),
    ((2, 1),),
    ((0, 0),),
    ((1, 1), (3, 1)),
    ((0, 1),),
    ((2, 2), (3, 2), (1, 2)),
    ((0, 2),),
)
MESH = pl.DeviceIdType.MESH
BF16 = jnp.bfloat16
F32 = jnp.float32


def kernel(
    act,
    cot,
    params,
    first,
    second,
    anchor,
    outer,
    merged_out,
    first_out,
    grad_out,
    acts,
    cots,
    scaled,
    partial,
    landed,
    relay,
    back,
    weights,
    state,
    seconds,
    mixed,
    rounded,
    got_a,
    sum_a,
    sent_b,
    got_b,
    total,
    near_sem,
    far_sem,
    local_sem,
    cot_s,
    cot_r,
    act_s,
    act_r,
    w_s,
    w_r,
    part_s,
    part_r,
    back_s,
    back_r,
    a_s,
    a_r,
    b_s,
    b_r,
    d_s,
    d_r,
    out_sem,
):
    replica = lax.axis_index("replica")
    shard = lax.axis_index("fsdp")
    y, p = shard // LINE, shard % LINE
    group, m = replica // CHIPS, replica % CHIPS
    core = replica % 2
    edge = (p == 0) | (p == LINE - 1)
    inner = (p == 1) | (p == 2)
    has_low, has_high = p > 0, p < LINE - 1
    upper = p // 2

    def mirrored(at):
        return at + upper * (LINE - 1 - 2 * at)

    is_end = 1 - (p + 1) % LINE // 2
    order = [mirrored(3), mirrored(2), mirrored(is_end), p]
    near = [p, mirrored(is_end), mirrored(2), mirrored(3)]
    ring = [lax.rem(y + j, RING) for j in range(RING)]
    chip = [lax.rem(m + j, CHIPS) for j in range(CHIPS)]
    swaps = [group + 1 - 2 * (group % 2), GROUPS - 1 - group]

    def on_ring(j):
        return {"fsdp": ring[j] * LINE + p}

    def on_line(at):
        return {"fsdp": y * LINE + at}

    def on_chip(j):
        return {"replica": group * CHIPS + chip[j]}

    def on_group(step):
        return {"replica": swaps[step] * CHIPS + m}

    def remote(src, dst, send, recv, where):
        return pltpu.make_async_remote_copy(
            src_ref=src,
            dst_ref=dst,
            send_sem=send,
            recv_sem=recv,
            device_id=where,
            device_id_type=MESH,
        )

    def rows_of(at, size):
        return pl.ds(pl.multiple_of(at * size, size), size)

    def features(ring_at, line_at):
        return pl.ds(pl.multiple_of(ring_at * SPAN + line_at * ROWS, ROWS), ROWS)

    def columns(half):
        return pl.ds(half * WIDE, WIDE)

    barrier = pltpu.get_barrier_semaphore()

    def signal(semaphore, where):
        pl.semaphore_signal(semaphore, inc=1, device_id=where, device_id_type=MESH)

    gate = replica - core + 1
    for j in range(1, RING):
        signal(barrier, {"replica": gate, "fsdp": ring[j] * LINE + p})

    @pl.when(has_low)
    def _():
        signal(barrier, {"replica": gate, "fsdp": shard - 1})

    @pl.when(has_high)
    def _():
        signal(barrier, {"replica": gate, "fsdp": shard + 1})

    for j in range(2, CHIPS, 2):
        signal(barrier, {"replica": group * CHIPS + lax.rem(m - core + j, CHIPS) + 1})

    @pl.when(core == 0)
    def _():
        signal(barrier, {"replica": gate})

    own_rows = rows_of(y, TOKENS)
    first_load = pltpu.make_async_copy(params, weights, local_sem.at[0])
    first_load.start()
    loads = [pltpu.make_async_copy(cot, cots.at[own_rows], local_sem.at[1])]
    for k in range(LINE):
        loads.append(
            pltpu.make_async_copy(
                act.at[:, features(y, order[k])], acts.at[k, own_rows], local_sem.at[2]
            )
        )
    loads += [
        pltpu.make_async_copy(anchor, state.at[0], local_sem.at[3]),
        pltpu.make_async_copy(outer, state.at[1], local_sem.at[3]),
        pltpu.make_async_copy(first, state.at[2], local_sem.at[3]),
        pltpu.make_async_copy(second, seconds, local_sem.at[4]),
    ]
    for load in loads:
        load.start()

    def await_bytes(like, semaphore):
        pltpu.make_async_copy(like, like, semaphore).wait()

    with jax.named_scope("scale"):
        first_load.wait()
        scaled[p] = (weights[...] * FACTOR).astype(BF16)
        rounded[...] = weights[...].astype(BF16)

    loads[0].wait()
    with jax.named_scope("gate"):

        @pl.when(core == 1)
        def _():
            pl.semaphore_wait(barrier, 2 * (RING - 1) + (CHIPS - 2) + 1 + 2 * (2 - is_end))
            signal(near_sem, {"replica": gate - 1})

        @pl.when(core == 0)
        def _():
            pl.semaphore_wait(near_sem, 1)
            for step in range(2):
                signal(barrier, on_group(step))

            @pl.when(group == 0)
            def _():
                signal(barrier, {"replica": 2 * CHIPS + m})

    def await_far():
        @pl.when(core == 0)
        def _():
            pl.semaphore_wait(barrier, 2 + jnp.where(group == 2, 1, 0))
            signal(far_sem, {"replica": gate})

        @pl.when(core == 1)
        def _():
            pl.semaphore_wait(far_sem, 1)

    def cot_copy(src, owner, half, slot, j):
        return remote(
            src, cots.at[rows_of(owner, TOKENS), columns(half)], cot_s, cot_r.at[slot], on_ring(j)
        )

    def cot_own(half, slot, j):
        return cot_copy(cots.at[own_rows, columns(half)], y, half, slot, j)

    def cot_passed(half, slot, j):
        owner = ring[RING - j]
        src = cots.at[rows_of(owner, TOKENS), columns(half)]
        return cot_copy(src, owner, half, slot, j)

    cot_copies = [
        cot_own(0, 0, 1),
        cot_own(1, 1, RING - 1),
        cot_own(1, 2, 1),
        cot_own(0, 3, RING - 1),
    ]
    cot_relays = [cot_passed(0, 4, 1), cot_passed(1, 5, RING - 1)]
    act_copies = [
        [
            remote(
                act.at[:, features(ring[j], order[k])],
                acts.at[k, own_rows],
                act_s,
                act_r.at[k],
                on_ring(j),
            )
            for j in range(1, RING)
        ]
        for k in range(LINE)
    ]
    a_copies = [
        remote(
            rounded.at[rows_of(chip[j], CHUNK)],
            got_a.at[j],
            a_s,
            a_r,
            on_chip(j),
        )
        for j in range(1, CHIPS)
    ]
    def b_copy(step, slot, to):
        where = {"replica": to * CHIPS + m}
        return remote(sent_b.at[step], got_b.at[slot], b_s, b_r.at[slot], where)

    d_copies = [
        remote(total.at[m], total.at[m], d_s, d_r, on_chip(j)) for j in range(1, CHIPS)
    ]

    def w_copy(block, half, way, to):
        rows = scaled.at[block, pl.ds(half * HALF, HALF)]
        return remote(rows, rows, w_s, w_r.at[block, half], on_line(to))

    def part_copy(k, half, way, to):
        slot = part_slot(way, order[k], to)
        return remote(
            relay.at[k, half], landed.at[slot, half], part_s, part_r.at[slot, half], on_line(to)
        )

    def part_slot(way, block, at):
        return jnp.where(block == at, LINE, block) if way == 1 else block

    def part_wait(way, block, half):
        slot = part_slot(way, block, p)
        await_bytes(landed.at[slot, half], part_r.at[slot, half])
        return landed[slot, half].astype(F32)

    def back_copy(i, j):
        return remote(
            back.at[i, rows_of(ring[j], TOKENS)],
            grad_out.at[:, features(y, near[i])],
            back_s,
            back_r,
            on_ring(j),
        )

    def back_own(i):
        return pltpu.make_async_copy(
            back.at[i, own_rows], grad_out.at[:, features(y, near[i])], out_sem
        )

    def w_start(half):
        @pl.when(has_low)
        def _():
            w_copy(p, half, 1, p - 1).start()

        @pl.when(has_high)
        def _():
            w_copy(p, half, 0, p + 1).start()

    for copy in a_copies:
        copy.start()
    for half in range(2):
        w_start(half)
    for copy in cot_copies + act_copies[0]:
        copy.start()

    def pass_near(half):
        @pl.when(inner)
        def _():
            w_copy(p - 1, half, 0, p + 1).wait_recv()
            w_copy(p - 1, half, 0, p + 1).start()
            w_copy(p + 1, half, 1, p - 1).wait_recv()
            w_copy(p + 1, half, 1, p - 1).start()

    def pass_far(half):
        @pl.when(p == 1)
        def _():
            w_copy(3, half, 1, 0).wait_recv()
            w_copy(3, half, 1, 0).start()

        @pl.when(p == 2)
        def _():
            w_copy(0, half, 0, 3).wait_recv()
            w_copy(0, half, 0, 3).start()

    def at_end_wait(block):
        @pl.when(edge)
        def _():
            for half in range(2):
                w_copy(block, half, 0, p).wait_recv()

    def input_grad(i):
        with jax.named_scope("ig%d" % i):
            if i > 0:
                at_end_wait(near[i])
            back[i] = lax.dot_general(
                cots[...],
                scaled[near[i]],
                (((1,), (1,)), ((), ())),
                preferred_element_type=F32,
            ).astype(BF16)
            for j in range(1, RING):
                back_copy(i, j).start()
            back_own(i).start()

    def product(k, half):
        partial[k, :, columns(half)] = lax.dot_general(
            acts[k],
            cots[:, columns(half)],
            (((0,), (0,)), ((), ())),
            preferred_element_type=F32,
        )
        if k == LINE - 1:
            return

        @pl.when(edge)
        def _():
            relay[k, half] = partial[k, :, columns(half)].astype(BF16)

        @pl.when(p == 0)
        def _():
            part_copy(k, half, 0, 1).start()

        @pl.when(p == LINE - 1)
        def _():
            part_copy(k, half, 1, LINE - 2).start()

    others = pl.ds(0, (RING - 1) * TOKENS)

    def cot_wait(slot):
        await_bytes(cots.at[pl.ds(0, TOKENS), columns(0)], cot_r.at[slot])

    def act_wait(k):
        await_bytes(acts.at[k, others], act_r.at[k])

    def gradient(k):
        with jax.named_scope("grad%d" % k):
            act_wait(k)
            product(k, 0)
            product(k, 1)

    def pass_part(k, half):
        def onward(way, to):
            both = partial[k, :, columns(half)] + part_wait(way, order[k], half)
            relay[k, half] = both.astype(BF16)
            part_copy(k, half, way, to).start()

        with jax.named_scope("part%d%d" % (k, half)):

            @pl.when(inner & (order[k] > p))
            def _():
                onward(0, p + 1)

            @pl.when(inner & (order[k] < p))
            def _():
                onward(1, p - 1)

    def outer_add(slot):
        b_copy(0, slot, swaps[0]).wait_recv()
        sum_a[...] += got_b[slot].astype(F32)

    def outer_step(step):
        if step == 0:
            await_far()
            b_copy(0, 0, swaps[0]).start()

            @pl.when(late)
            def _():
                b_copy(0, group - 1, 0).start()

        elif step == 1:
            outer_add(0)

            @pl.when(group < 3)
            def _():
                sent_b[1] = sum_a[...].astype(BF16)
                b_copy(1, 1, swaps[1]).start()

        else:

            @pl.when(group == 0)
            def _():
                outer_add(2)

            outer_add(1)
            total[m] = sum_a[...].astype(BF16)
            for copy in d_copies:
                copy.start()

    late = group > 1

    def outer_at(place):
        with jax.named_scope("outer_%d" % place):
            for member, step in SWAPS_AT[place]:

                @pl.when(group == member)
                def _():
                    outer_step(step)

    with jax.named_scope("cot_relay"):
        for slot in range(2):
            cot_wait(slot)
            cot_relays[slot].start()
    for copies in act_copies[1:]:
        for copy in copies:
            copy.start()
    with jax.named_scope("sum_a"):
        await_bytes(got_a.at[pl.ds(1, CHIPS - 1)], a_r)
        own_sum = weights[rows_of(m, CHUNK)]
        for j in range(1, CHIPS):
            own_sum += got_a[j].astype(F32)
        sum_a[...] = own_sum
        sent_b[0] = own_sum.astype(BF16)
    outer_at(0)
    with jax.named_scope("pass_near0"):
        pass_near(0)
    with jax.named_scope("pass_near1"):
        pass_near(1)
    outer_at(1)
    with jax.named_scope("grad00"):
        await_bytes(scaled.at[0], local_sem.at[2])
        cot_wait(3)
        cot_wait(4)
        act_wait(0)
        product(0, 0)
    with jax.named_scope("pass_far0"):
        pass_far(0)
    outer_at(2)
    with jax.named_scope("grad01"):
        cot_wait(2)
        cot_wait(5)
        product(0, 1)
    input_grad(0)
    outer_at(3)
    with jax.named_scope("pass_far1"):
        pass_far(1)
    pass_part(0, 0)
    input_grad(1)
    gradient(1)
    pass_part(0, 1)
    outer_at(4)
    gradient(2)
    input_grad(2)

    @pl.when(inner)
    def _():
        input_grad(3)

    outer_at(5)
    pass_part(2, 0)
    pass_part(1, 0)
    outer_at(6)
    gradient(3)
    pass_part(2, 1)
    pass_part(1, 1)
    outer_at(7)

    @pl.when(edge)
    def _():
        input_grad(3)

    with jax.named_scope("outer"):
        await_bytes(scaled.at[pl.ds(0, 3)], local_sem.at[3])
        loads[-1].wait()
        await_bytes(total.at[pl.ds(0, CHIPS - 1)], d_r)
        mean = total[...].astype(F32).reshape(ROWS, KVW) * (1.0 / REPLICAS)
        old = state[0].astype(F32)
        outer_grad = old - mean
        moment = OUTER_MOMENT * state[1].astype(F32) + outer_grad
        new = old - OUTER_RATE * (outer_grad + OUTER_MOMENT * moment)
        kept = MIXING * (1.0 - INNER_RATE * WEIGHT_DECAY)
        mixed[...] = kept * weights[...] + (1.0 - MIXING) * new

    for half in range(2):
        cut = columns(half)
        with jax.named_scope("last%d" % half):

            @pl.when(has_low)
            def _():
                partial[3, :, cut] += part_wait(0, p, half)

            @pl.when(has_high)
            def _():
                partial[3, :, cut] += part_wait(1, p, half)

            gradient_now = partial[3, :, cut] * FACTOR
            moment = BETA_FIRST * state[2, :, cut].astype(F32) + (1.0 - BETA_FIRST) * gradient_now
            spread = (
                BETA_SECOND * seconds[:, cut] + (1.0 - BETA_SECOND) * gradient_now * gradient_now
            )
            step = moment / (jnp.sqrt(spread) + EPSILON)
            first_out[:, cut] = moment
            merged_out[:, cut] = mixed[:, cut] - (MIXING * INNER_RATE) * step

    with jax.named_scope("drain_back"):
        three = landed.at[pl.ds(0, 3)]
        await_bytes(three, back_r)
    with jax.named_scope("drain"):
        await_bytes(scaled.at[0], out_sem)
        await_bytes(three, back_s)
        await_bytes(three, act_s)
        await_bytes(three, part_s)
        await_bytes(landed.at[pl.ds(0, 3), 0], cot_s)
        await_bytes(got_a.at[pl.ds(1, CHIPS - 1)], a_s)
        await_bytes(total.at[pl.ds(0, CHIPS - 1)], d_s)
        await_bytes(sent_b, b_s)

        @pl.when(group == 2)
        def _():
            await_bytes(sent_b.at[0], b_s)


        @pl.when(edge)
        def _():
            await_bytes(scaled.at[0], w_s)

        @pl.when(inner)
        def _():
            await_bytes(landed, w_s)


def write_out(merged, first, grad, merged_out, first_out, grad_out, sem):
    copies = [
        pltpu.make_async_copy(merged, merged_out, sem.at[0]),
        pltpu.make_async_copy(first, first_out, sem.at[1]),
        pltpu.make_async_copy(grad, grad_out, sem.at[2]),
    ]
    for copy in copies:
        copy.start()
    for copy in copies:
        copy.wait()


def on_device(activations, cotangent, params, first_moment, second_moment, anchor, outer_momentum):
    any_spec = pl.BlockSpec(memory_space=pl.ANY)
    vmem_spec = pl.BlockSpec(memory_space=pltpu.VMEM)
    dma = pltpu.SemaphoreType.DMA
    results = (
        jax.ShapeDtypeStruct((ROWS, KVW), F32),
        jax.ShapeDtypeStruct((ROWS, KVW), F32),
        jax.ShapeDtypeStruct((TOKENS, D), BF16),
    )
    held = pl.pallas_call(
        kernel,
        out_shape=tuple(pltpu.VMEM(r.shape, r.dtype) for r in results),
        in_specs=[any_spec] * 7,
        out_specs=(vmem_spec,) * 3,
        scratch_shapes=[
            pltpu.VMEM((LINE, RING * TOKENS, ROWS), BF16),
            pltpu.VMEM((RING * TOKENS, KVW), BF16),
            pltpu.VMEM((LINE, ROWS, KVW), BF16),
            pltpu.VMEM((LINE, ROWS, KVW), F32),
            pltpu.VMEM((LINE + 1, 2, ROWS, WIDE), BF16),
            pltpu.VMEM((LINE - 1, 2, ROWS, WIDE), BF16),
            pltpu.VMEM((LINE, RING * TOKENS, ROWS), BF16),
            pltpu.VMEM((ROWS, KVW), F32),
            pltpu.VMEM((3, ROWS, KVW), BF16),
            pltpu.VMEM((ROWS, KVW), F32),
            pltpu.VMEM((ROWS, KVW), F32),
            pltpu.VMEM((ROWS, KVW), BF16),
            pltpu.VMEM((CHIPS, CHUNK, KVW), BF16),
            pltpu.VMEM((CHUNK, KVW), F32),
            pltpu.VMEM((2, CHUNK, KVW), BF16),
            pltpu.VMEM((3, CHUNK, KVW), BF16),
            pltpu.VMEM((CHIPS, CHUNK, KVW), BF16),
            pltpu.SemaphoreType.REGULAR,
            pltpu.SemaphoreType.REGULAR,
            dma((5,)),
            dma,
            dma((6,)),
            dma,
            dma((LINE,)),
            dma,
            dma((LINE, 2)),
            dma,
            dma((LINE + 1, 2)),
            dma,
            dma,
            dma,
            dma,
            dma,
            dma((3,)),
            dma,
            dma,
            dma,
        ],
        compiler_params=pltpu.CompilerParams(
            collective_id=0, has_side_effects=True, vmem_limit_bytes=58 * 2**20
        ),
        name="diloco_step",
    )(
        activations[0, 0],
        cotangent[0, 0],
        params[0],
        first_moment[0],
        second_moment[0],
        anchor,
        outer_momentum,
    )
    merged, first, grad = pl.pallas_call(
        write_out,
        out_shape=results,
        in_specs=[vmem_spec] * 3,
        out_specs=(any_spec,) * 3,
        scratch_shapes=[dma((3,))],
        name="write_out",
    )(*(pltpu.with_memory_space_constraint(x, pltpu.VMEM) for x in held))
    return merged[None], first[None], grad[None, None]


def solution(mesh):
    placed = (
        P("replica", None, "fsdp", None),
        P("replica", None, "fsdp", None),
        P("replica", "fsdp", None),
        P("replica", "fsdp", None),
        P("replica", "fsdp", None),
        P("fsdp", None),
        P("fsdp", None),
    )
    return jax.shard_map(
        on_device,
        mesh=mesh,
        in_specs=placed,
        out_specs=(
            P("replica", "fsdp", None),
            P("replica", "fsdp", None),
            P("replica", None, "fsdp", None),
        ),
        check_vma=False,
    )
```

```python
import jax
import jax.numpy as jnp
from jax import lax
from jax.experimental import pallas as pl
from jax.experimental.pallas import tpu as pltpu
from jax.sharding import PartitionSpec as P

D = 4096
KVW = 512
ROWS = 256
TOKENS = 128
RING = 4
LINE = 4
GROUPS = 4
SPAN = ROWS * LINE
HALF = ROWS // 2
WIDE = KVW // 2
CHIPS = 8
CHUNK = ROWS // CHIPS
REPLICAS = 32
PIECES = 1

BETA_FIRST = 0.9
BETA_SECOND = 0.95
EPSILON = 1e-08
WEIGHT_DECAY = 0.1
INNER_RATE = 0.03
OUTER_RATE = 0.7
OUTER_MOMENT = 0.9
MIXING = 0.5

FACTOR = float(D) ** (-0.5)
ALL, ENDS, INSIDE, FOOT, ABOVE = range(5)
SWAPS_AT = (
    ((2, 0, ALL), (3, 0, ALL)),
    ((1, 0, ALL),),
    ((3, 1, FOOT),),
    ((2, 1, ALL), (3, 1, ABOVE)),
    ((0, 0, ALL),),
    ((1, 1, ALL), (0, 1, ENDS)),
    ((0, 1, INSIDE),),
    ((2, 2, ALL), (3, 2, ALL), (1, 2, ALL)),
    ((0, 2, ALL),),
)
MESH = pl.DeviceIdType.MESH
BF16 = jnp.bfloat16
F32 = jnp.float32


def kernel(
    act,
    cot,
    params,
    first,
    second,
    anchor,
    outer,
    merged_out,
    first_out,
    grad_out,
    acts,
    cots,
    scaled,
    partial,
    landed,
    relay,
    back,
    weights,
    state,
    seconds,
    mixed,
    rounded,
    got_a,
    sum_a,
    sent_b,
    got_b,
    total,
    near_sem,
    far_sem,
    local_sem,
    cot_s,
    cot_r,
    act_s,
    act_r,
    w_s,
    w_r,
    part_s,
    part_r,
    back_s,
    back_r,
    a_s,
    a_r,
    b_s,
    b_r,
    d_s,
    d_r,
    out_sem,
):
    replica = lax.axis_index("replica")
    shard = lax.axis_index("fsdp")
    y, p = shard // LINE, shard % LINE
    group, m = replica // CHIPS, replica % CHIPS
    core = replica % 2
    edge = (p == 0) | (p == LINE - 1)
    inner = (p == 1) | (p == 2)
    has_low, has_high = p > 0, p < LINE - 1
    upper = p // 2

    def mirrored(at):
        return at + upper * (LINE - 1 - 2 * at)

    is_end = 1 - (p + 1) % LINE // 2
    order = [mirrored(3), mirrored(2), mirrored(is_end), p]
    near = [p, mirrored(is_end), mirrored(2), mirrored(3)]
    ring = [lax.rem(y + j, RING) for j in range(RING)]
    chip = [lax.rem(m + j, CHIPS) for j in range(CHIPS)]
    swaps = [group + 1 - 2 * (group % 2), GROUPS - 1 - group]

    def on_ring(j):
        return {"fsdp": ring[j] * LINE + p}

    def on_line(at):
        return {"fsdp": y * LINE + at}

    def on_chip(j):
        return {"replica": group * CHIPS + chip[j]}

    def on_group(step):
        return {"replica": swaps[step] * CHIPS + m}

    def remote(src, dst, send, recv, where):
        return pltpu.make_async_remote_copy(
            src_ref=src,
            dst_ref=dst,
            send_sem=send,
            recv_sem=recv,
            device_id=where,
            device_id_type=MESH,
        )

    def rows_of(at, size):
        return pl.ds(pl.multiple_of(at * size, size), size)

    def features(ring_at, line_at):
        return pl.ds(pl.multiple_of(ring_at * SPAN + line_at * ROWS, ROWS), ROWS)

    def columns(half):
        return pl.ds(half * WIDE, WIDE)

    barrier = pltpu.get_barrier_semaphore()

    def signal(semaphore, where):
        pl.semaphore_signal(semaphore, inc=1, device_id=where, device_id_type=MESH)

    gate = replica - core + 1
    for j in range(1, RING):
        signal(barrier, {"replica": gate, "fsdp": ring[j] * LINE + p})

    @pl.when(has_low)
    def _():
        signal(barrier, {"replica": gate, "fsdp": shard - 1})

    @pl.when(has_high)
    def _():
        signal(barrier, {"replica": gate, "fsdp": shard + 1})

    for j in range(2, CHIPS, 2):
        signal(barrier, {"replica": group * CHIPS + lax.rem(m - core + j, CHIPS) + 1})

    @pl.when(core == 0)
    def _():
        signal(barrier, {"replica": gate})

    own_rows = rows_of(y, TOKENS)
    first_load = pltpu.make_async_copy(params, weights, local_sem.at[0])
    first_load.start()
    loads = [pltpu.make_async_copy(cot, cots.at[own_rows], local_sem.at[1])]
    for k in range(LINE):
        loads.append(
            pltpu.make_async_copy(
                act.at[:, features(y, order[k])], acts.at[k, own_rows], local_sem.at[2]
            )
        )
    loads += [
        pltpu.make_async_copy(anchor, state.at[0], local_sem.at[3]),
        pltpu.make_async_copy(outer, state.at[1], local_sem.at[3]),
        pltpu.make_async_copy(first, state.at[2], local_sem.at[3]),
        pltpu.make_async_copy(second, seconds, local_sem.at[4]),
    ]
    for load in loads:
        load.start()

    def await_bytes(like, semaphore):
        pltpu.make_async_copy(like, like, semaphore).wait()

    with jax.named_scope("scale"):
        first_load.wait()
        scaled[p] = (weights[...] * FACTOR).astype(BF16)
        rounded[...] = weights[...].astype(BF16)

    loads[0].wait()
    with jax.named_scope("gate"):

        @pl.when(core == 1)
        def _():
            pl.semaphore_wait(barrier, 2 * (RING - 1) + (CHIPS - 2) + 1 + 2 * (2 - is_end))
            signal(near_sem, {"replica": gate - 1})

        @pl.when(core == 0)
        def _():
            pl.semaphore_wait(near_sem, 1)
            for step in range(2):
                signal(barrier, on_group(step))
    def await_far():
        @pl.when(core == 0)
        def _():
            pl.semaphore_wait(barrier, 2)
            signal(far_sem, {"replica": gate})

        @pl.when(core == 1)
        def _():
            pl.semaphore_wait(far_sem, 1)

    def cot_copy(src, owner, half, slot, j):
        return remote(
            src, cots.at[rows_of(owner, TOKENS), columns(half)], cot_s, cot_r.at[slot], on_ring(j)
        )

    def cot_own(half, slot, j):
        return cot_copy(cots.at[own_rows, columns(half)], y, half, slot, j)

    def cot_passed(half, slot, j):
        owner = ring[RING - j]
        src = cots.at[rows_of(owner, TOKENS), columns(half)]
        return cot_copy(src, owner, half, slot, j)

    cot_copies = [
        cot_own(0, 0, 1),
        cot_own(1, 1, RING - 1),
        cot_own(1, 2, 1),
        cot_own(0, 3, RING - 1),
    ]
    cot_relays = [cot_passed(0, 4, 1), cot_passed(1, 5, RING - 1)]
    def act_copy(k, part, j):
        if k == 0:
            start = pl.multiple_of(ring[j] * SPAN + order[0] * ROWS + part * HALF, HALF)
            src, dst = pl.ds(start, HALF), pl.ds(part * HALF, HALF)
        else:
            src, dst = features(ring[j], order[k]), pl.ds(0, ROWS)
        return remote(
            act.at[:, src], acts.at[k, own_rows, dst], act_s, act_r.at[k + part], on_ring(j)
        )

    act_parts = [(0, 0), (0, 1), (1, 1), (2, 1), (3, 1)]
    act_copies = [[act_copy(k, part, j) for j in range(1, RING)] for k, part in act_parts]
    a_copies = [
        remote(
            rounded.at[rows_of(chip[j], CHUNK)],
            got_a.at[j],
            a_s,
            a_r,
            on_chip(j),
        )
        for j in range(1, CHIPS)
    ]
    def b_copy(step, slot, to):
        where = {"replica": to * CHIPS + m}
        return remote(sent_b.at[step], got_b.at[slot], b_s, b_r.at[slot], where)

    d_copies = [
        remote(total.at[m], total.at[m], d_s, d_r, on_chip(j)) for j in range(1, CHIPS)
    ]

    def w_copy(block, half, way, to):
        rows = scaled.at[block, pl.ds(half * HALF, HALF)]
        return remote(rows, rows, w_s, w_r.at[block, half], on_line(to))

    def part_copy(k, half, way, to):
        slot = part_slot(way, order[k], to)
        return remote(
            relay.at[k, half], landed.at[slot, half], part_s, part_r.at[slot, half], on_line(to)
        )

    def part_slot(way, block, at):
        return jnp.where(block == at, LINE, block) if way == 1 else block

    def part_wait(way, block, half):
        slot = part_slot(way, block, p)
        await_bytes(landed.at[slot, half], part_r.at[slot, half])
        return landed[slot, half].astype(F32)

    def back_copy(i, j):
        return remote(
            back.at[i, rows_of(ring[j], TOKENS)],
            grad_out.at[:, features(y, near[i])],
            back_s,
            back_r,
            on_ring(j),
        )

    def back_own(i):
        return pltpu.make_async_copy(
            back.at[i, own_rows], grad_out.at[:, features(y, near[i])], out_sem
        )

    def w_start(half):
        @pl.when(has_low)
        def _():
            w_copy(p, half, 1, p - 1).start()

        @pl.when(has_high)
        def _():
            w_copy(p, half, 0, p + 1).start()

    for copy in a_copies:
        copy.start()
    for half in range(2):
        w_start(half)
    for copy in cot_copies + act_copies[0]:
        copy.start()

    def pass_near(half):
        @pl.when(inner)
        def _():
            w_copy(p - 1, half, 0, p + 1).wait_recv()
            w_copy(p - 1, half, 0, p + 1).start()
            w_copy(p + 1, half, 1, p - 1).wait_recv()
            w_copy(p + 1, half, 1, p - 1).start()

    def pass_far(half):
        @pl.when(p == 1)
        def _():
            w_copy(3, half, 1, 0).wait_recv()
            w_copy(3, half, 1, 0).start()

        @pl.when(p == 2)
        def _():
            w_copy(0, half, 0, 3).wait_recv()
            w_copy(0, half, 0, 3).start()

    def at_end_wait(block):
        @pl.when(edge)
        def _():
            for half in range(2):
                w_copy(block, half, 0, p).wait_recv()

    def input_grad(i):
        with jax.named_scope("ig%d" % i):
            if i > 0:
                at_end_wait(near[i])
            back[i] = lax.dot_general(
                cots[...],
                scaled[near[i]],
                (((1,), (1,)), ((), ())),
                preferred_element_type=F32,
            ).astype(BF16)
            for j in range(1, RING):
                back_copy(i, j).start()
            back_own(i).start()

    def rows(half):
        return pl.ds(half * HALF, HALF)

    def product(k, half):
        partial[k, rows(half)] = lax.dot_general(
            acts[k, :, rows(half)],
            cots[...],
            (((0,), (0,)), ((), ())),
            preferred_element_type=F32,
        )
        if k == LINE - 1:
            return

        @pl.when(edge)
        def _():
            relay[k, half] = partial[k, rows(half)].astype(BF16)

        @pl.when(p == 0)
        def _():
            part_copy(k, half, 0, 1).start()

        @pl.when(p == LINE - 1)
        def _():
            part_copy(k, half, 1, LINE - 2).start()

    others = pl.ds(0, (RING - 1) * TOKENS)

    def cot_wait(slot):
        await_bytes(cots.at[pl.ds(0, TOKENS), columns(0)], cot_r.at[slot])

    def act_wait(k, part=1):
        width = HALF if k == 0 else ROWS
        await_bytes(acts.at[k, others, pl.ds(0, width)], act_r.at[k + part])

    def gradient(k):
        with jax.named_scope("grad%d" % k):
            act_wait(k)
            product(k, 0)
            product(k, 1)

    def pass_part(k, half):
        def onward(way, to):
            both = partial[k, rows(half)] + part_wait(way, order[k], half)
            relay[k, half] = both.astype(BF16)
            part_copy(k, half, way, to).start()

        with jax.named_scope("part%d%d" % (k, half)):

            @pl.when(inner & (order[k] > p))
            def _():
                onward(0, p + 1)

            @pl.when(inner & (order[k] < p))
            def _():
                onward(1, p - 1)

    def outer_add(slot):
        b_copy(0, slot, swaps[0]).wait_recv()
        sum_a[...] += got_b[slot].astype(F32)

    def outer_step(step):
        if step == 0:
            await_far()
            b_copy(0, 0, swaps[0]).start()

        elif step == 1:
            outer_add(0)
            sent_b[1] = sum_a[...].astype(BF16)
            b_copy(1, 1, swaps[1]).start()

        else:

            outer_add(1)
            total[m] = sum_a[...].astype(BF16)
            for copy in d_copies:
                copy.start()

    late = group > 1

    def outer_at(place):
        with jax.named_scope("outer_%d" % place):
            for member, step, where in SWAPS_AT[place]:

                @pl.when((group == member) & (True, edge, inner, p == 0, has_low)[where])
                def _():
                    outer_step(step)

    with jax.named_scope("cot_relay"):
        for slot in range(2):
            cot_wait(slot)
            cot_relays[slot].start()
    for copies in act_copies[1:]:
        for copy in copies:
            copy.start()
    with jax.named_scope("sum_a"):
        await_bytes(got_a.at[pl.ds(1, CHIPS - 1)], a_r)
        own_sum = weights[rows_of(m, CHUNK)]
        for j in range(1, CHIPS):
            own_sum += got_a[j].astype(F32)
        sum_a[...] = own_sum
        sent_b[0] = own_sum.astype(BF16)
    outer_at(0)
    with jax.named_scope("pass_near0"):
        pass_near(0)
    with jax.named_scope("pass_near1"):
        pass_near(1)
    outer_at(1)
    outer_at(2)
    with jax.named_scope("grad00"):
        await_bytes(scaled.at[0], local_sem.at[2])
        for slot in range(2, 6):
            cot_wait(slot)
        act_wait(0, 0)
        product(0, 0)
    with jax.named_scope("grad01"):
        act_wait(0, 1)
        product(0, 1)
    outer_at(3)
    with jax.named_scope("pass_far0"):
        pass_far(0)
    input_grad(0)
    outer_at(4)
    with jax.named_scope("pass_far1"):
        pass_far(1)
    pass_part(0, 0)
    input_grad(1)
    gradient(1)
    pass_part(0, 1)
    outer_at(5)
    gradient(2)
    input_grad(2)

    @pl.when(inner)
    def _():
        input_grad(3)

    outer_at(6)
    pass_part(2, 0)
    pass_part(1, 0)
    outer_at(7)
    gradient(3)
    pass_part(2, 1)
    outer_at(8)
    pass_part(1, 1)

    @pl.when(edge)
    def _():
        input_grad(3)

    with jax.named_scope("outer"):
        await_bytes(scaled.at[pl.ds(0, 3)], local_sem.at[3])
        loads[-1].wait()
        await_bytes(total.at[pl.ds(0, CHIPS - 1)], d_r)
        mean = total[...].astype(F32).reshape(ROWS, KVW) * (1.0 / REPLICAS)
        old = state[0].astype(F32)
        outer_grad = old - mean
        moment = OUTER_MOMENT * state[1].astype(F32) + outer_grad
        new = old - OUTER_RATE * (outer_grad + OUTER_MOMENT * moment)
        kept = MIXING * (1.0 - INNER_RATE * WEIGHT_DECAY)
        mixed[...] = kept * weights[...] + (1.0 - MIXING) * new

    for half in range(2):
        cut = rows(half)
        with jax.named_scope("last%d" % half):

            @pl.when(has_low)
            def _():
                partial[3, cut] += part_wait(0, p, half)

            @pl.when(has_high)
            def _():
                partial[3, cut] += part_wait(1, p, half)

            gradient_now = partial[3, cut] * FACTOR
            moment = BETA_FIRST * state[2, cut].astype(F32) + (1.0 - BETA_FIRST) * gradient_now
            spread = (
                BETA_SECOND * seconds[cut] + (1.0 - BETA_SECOND) * gradient_now * gradient_now
            )
            step = moment / (jnp.sqrt(spread) + EPSILON)
            first_out[cut] = moment
            merged_out[cut] = mixed[cut] - (MIXING * INNER_RATE) * step

    with jax.named_scope("drain_back"):
        three = landed.at[pl.ds(0, 3)]
        await_bytes(three, back_r)
    with jax.named_scope("drain"):
        await_bytes(scaled.at[0], out_sem)
        await_bytes(three, back_s)
        await_bytes(three, act_s)
        await_bytes(three, part_s)
        await_bytes(landed.at[pl.ds(0, 3), 0], cot_s)
        await_bytes(got_a.at[pl.ds(1, CHIPS - 1)], a_s)
        await_bytes(total.at[pl.ds(0, CHIPS - 1)], d_s)
        await_bytes(sent_b, b_s)

        @pl.when(edge)
        def _():
            await_bytes(scaled.at[0], w_s)

        @pl.when(inner)
        def _():
            await_bytes(landed, w_s)


def write_out(merged, first, grad, merged_out, first_out, grad_out, sem):
    copies = []
    for src, dst in ((grad, grad_out), (merged, merged_out), (first, first_out)):
        size = src.shape[0] // PIECES
        for i in range(PIECES):
            cut = pl.ds(i * size, size)
            copies.append(pltpu.make_async_copy(src.at[cut], dst.at[cut], sem.at[len(copies)]))
    for copy in copies:
        copy.start()
    for copy in copies:
        copy.wait()


def on_device(activations, cotangent, params, first_moment, second_moment, anchor, outer_momentum):
    any_spec = pl.BlockSpec(memory_space=pl.ANY)
    vmem_spec = pl.BlockSpec(memory_space=pltpu.VMEM)
    dma = pltpu.SemaphoreType.DMA
    results = (
        jax.ShapeDtypeStruct((ROWS, KVW), F32),
        jax.ShapeDtypeStruct((ROWS, KVW), F32),
        jax.ShapeDtypeStruct((TOKENS, D), BF16),
    )
    held = pl.pallas_call(
        kernel,
        out_shape=tuple(pltpu.VMEM(r.shape, r.dtype) for r in results),
        in_specs=[any_spec] * 7,
        out_specs=(vmem_spec,) * 3,
        scratch_shapes=[
            pltpu.VMEM((LINE, RING * TOKENS, ROWS), BF16),
            pltpu.VMEM((RING * TOKENS, KVW), BF16),
            pltpu.VMEM((LINE, ROWS, KVW), BF16),
            pltpu.VMEM((LINE, ROWS, KVW), F32),
            pltpu.VMEM((LINE + 1, 2, HALF, KVW), BF16),
            pltpu.VMEM((LINE - 1, 2, HALF, KVW), BF16),
            pltpu.VMEM((LINE, RING * TOKENS, ROWS), BF16),
            pltpu.VMEM((ROWS, KVW), F32),
            pltpu.VMEM((3, ROWS, KVW), BF16),
            pltpu.VMEM((ROWS, KVW), F32),
            pltpu.VMEM((ROWS, KVW), F32),
            pltpu.VMEM((ROWS, KVW), BF16),
            pltpu.VMEM((CHIPS, CHUNK, KVW), BF16),
            pltpu.VMEM((CHUNK, KVW), F32),
            pltpu.VMEM((2, CHUNK, KVW), BF16),
            pltpu.VMEM((3, CHUNK, KVW), BF16),
            pltpu.VMEM((CHIPS, CHUNK, KVW), BF16),
            pltpu.SemaphoreType.REGULAR,
            pltpu.SemaphoreType.REGULAR,
            dma((5,)),
            dma,
            dma((6,)),
            dma,
            dma((LINE + 1,)),
            dma,
            dma((LINE, 2)),
            dma,
            dma((LINE + 1, 2)),
            dma,
            dma,
            dma,
            dma,
            dma,
            dma((3,)),
            dma,
            dma,
            dma,
        ],
        compiler_params=pltpu.CompilerParams(
            collective_id=0, has_side_effects=True, vmem_limit_bytes=58 * 2**20
        ),
        name="diloco_step",
    )(
        activations[0, 0],
        cotangent[0, 0],
        params[0],
        first_moment[0],
        second_moment[0],
        anchor,
        outer_momentum,
    )
    merged, first, grad = pl.pallas_call(
        write_out,
        out_shape=results,
        in_specs=[vmem_spec] * 3,
        out_specs=(any_spec,) * 3,
        scratch_shapes=[dma((3 * PIECES,))],
        name="write_out",
    )(*(pltpu.with_memory_space_constraint(x, pltpu.VMEM) for x in held))
    return merged[None], first[None], grad[None, None]


def solution(mesh):
    placed = (
        P("replica", None, "fsdp", None),
        P("replica", None, "fsdp", None),
        P("replica", "fsdp", None),
        P("replica", "fsdp", None),
        P("replica", "fsdp", None),
        P("fsdp", None),
        P("fsdp", None),
    )
    return jax.shard_map(
        on_device,
        mesh=mesh,
        in_specs=placed,
        out_specs=(
            P("replica", "fsdp", None),
            P("replica", "fsdp", None),
            P("replica", None, "fsdp", None),
        ),
        check_vma=False,
    )
```

```python
import jax
import jax.numpy as jnp
from jax import lax
from jax.experimental import pallas as pl
from jax.experimental.pallas import tpu as pltpu
from jax.sharding import PartitionSpec as P

D = 4096
KVW = 512
ROWS = 256
TOKENS = 128
RING = 4
LINE = 4
GROUPS = 4
SPAN = ROWS * LINE
HALF = ROWS // 2
WIDE = KVW // 2
CHIPS = 8
CHUNK = ROWS // CHIPS
REPLICAS = 32
PIECES = 1

BETA_FIRST = 0.9
BETA_SECOND = 0.95
EPSILON = 1e-08
WEIGHT_DECAY = 0.1
INNER_RATE = 0.03
OUTER_RATE = 0.7
OUTER_MOMENT = 0.9
MIXING = 0.5

FACTOR = float(D) ** (-0.5)
ALL, ENDS, INSIDE, FOOT, ABOVE, CORE0, CORE1, INSIDE0, REST = range(9)
SWAPS_AT = (
    ((2, 0, ALL), (3, 0, ALL)),
    ((1, 0, ALL),),
    ((3, 1, FOOT),),
    ((2, 1, ALL), (3, 1, ABOVE)),
    ((0, 0, CORE0),),
    ((0, 0, CORE1), (1, 1, ALL), (0, 1, ENDS)),
    ((0, 1, INSIDE),),
    ((2, 2, ALL), (3, 2, ALL), (1, 2, ALL), (0, 2, INSIDE0)),
    ((0, 2, REST),),
)
MESH = pl.DeviceIdType.MESH
BF16 = jnp.bfloat16
F32 = jnp.float32


def kernel(
    act,
    cot,
    params,
    first,
    second,
    anchor,
    outer,
    merged_out,
    first_out,
    grad_out,
    acts,
    cots,
    scaled,
    partial,
    landed,
    relay,
    back,
    weights,
    state,
    seconds,
    mixed,
    rounded,
    got_a,
    sum_a,
    sent_b,
    got_b,
    total,
    near_sem,
    far_sem,
    local_sem,
    cot_s,
    cot_r,
    act_s,
    act_r,
    w_s,
    w_r,
    part_s,
    part_r,
    back_s,
    back_r,
    a_s,
    a_r,
    b_s,
    b_r,
    d_s,
    d_r,
    out_sem,
):
    replica = lax.axis_index("replica")
    shard = lax.axis_index("fsdp")
    y, p = shard // LINE, shard % LINE
    group, m = replica // CHIPS, replica % CHIPS
    core = replica % 2
    edge = (p == 0) | (p == LINE - 1)
    inner = (p == 1) | (p == 2)
    has_low, has_high = p > 0, p < LINE - 1
    upper = p // 2

    def mirrored(at):
        return at + upper * (LINE - 1 - 2 * at)

    is_end = 1 - (p + 1) % LINE // 2
    order = [mirrored(3), mirrored(2), mirrored(is_end), p]
    near = [p, mirrored(is_end), mirrored(2), mirrored(3)]
    ring = [lax.rem(y + j, RING) for j in range(RING)]
    chip = [lax.rem(m + j, CHIPS) for j in range(CHIPS)]
    swaps = [group + 1 - 2 * (group % 2), GROUPS - 1 - group]

    def on_ring(j):
        return {"fsdp": ring[j] * LINE + p}

    def on_line(at):
        return {"fsdp": y * LINE + at}

    def on_chip(j):
        return {"replica": group * CHIPS + chip[j]}

    def on_group(step):
        return {"replica": swaps[step] * CHIPS + m}

    def remote(src, dst, send, recv, where):
        return pltpu.make_async_remote_copy(
            src_ref=src,
            dst_ref=dst,
            send_sem=send,
            recv_sem=recv,
            device_id=where,
            device_id_type=MESH,
        )

    def rows_of(at, size):
        return pl.ds(pl.multiple_of(at * size, size), size)

    def features(ring_at, line_at):
        return pl.ds(pl.multiple_of(ring_at * SPAN + line_at * ROWS, ROWS), ROWS)

    def columns(half):
        return pl.ds(half * WIDE, WIDE)

    barrier = pltpu.get_barrier_semaphore()

    def signal(semaphore, where):
        pl.semaphore_signal(semaphore, inc=1, device_id=where, device_id_type=MESH)

    apart = group == 0
    hub = jnp.where(apart, 0, 1)
    hub_here = replica - core + hub
    sibling = {"replica": replica + 1 - 2 * core}
    near_gate = jnp.where(apart, replica, hub_here)
    for j in range(1, RING):
        signal(barrier, {"replica": near_gate, "fsdp": ring[j] * LINE + p})

    @pl.when(has_low)
    def _():
        signal(barrier, {"replica": near_gate, "fsdp": shard - 1})

    @pl.when(has_high)
    def _():
        signal(barrier, {"replica": near_gate, "fsdp": shard + 1})

    for j in range(2, CHIPS, 2):
        signal(barrier, {"replica": group * CHIPS + lax.rem(m - core + j, CHIPS) + hub})

    @pl.when(core != hub)
    def _():
        signal(barrier, sibling)

    own_rows = rows_of(y, TOKENS)
    first_load = pltpu.make_async_copy(params, weights, local_sem.at[0])
    first_load.start()
    loads = [pltpu.make_async_copy(cot, cots.at[own_rows], local_sem.at[1])]
    for k in range(LINE):
        loads.append(
            pltpu.make_async_copy(
                act.at[:, features(y, order[k])], acts.at[k, own_rows], local_sem.at[2]
            )
        )
    loads += [
        pltpu.make_async_copy(anchor, state.at[0], local_sem.at[3]),
        pltpu.make_async_copy(outer, state.at[1], local_sem.at[3]),
        pltpu.make_async_copy(first, state.at[2], local_sem.at[3]),
        pltpu.make_async_copy(second, seconds, local_sem.at[4]),
    ]
    for load in loads:
        load.start()

    def await_bytes(like, semaphore):
        pltpu.make_async_copy(like, like, semaphore).wait()

    with jax.named_scope("scale"):
        first_load.wait()
        scaled[p] = (weights[...] * FACTOR).astype(BF16)
        rounded[...] = weights[...].astype(BF16)

    loads[0].wait()
    with jax.named_scope("gate"):

        of_ring = (RING - 1) + (2 - is_end)
        of_chips = (CHIPS - 2) + 1
        met = jnp.where(apart, of_ring + (1 - core) * of_chips, 2 * of_ring + of_chips)

        @pl.when(apart | (core == 1))
        def _():
            pl.semaphore_wait(barrier, met)

        @pl.when(core == hub)
        def _():
            signal(near_sem, sibling)

        @pl.when((core == 0) & (group > 0))
        def _():
            pl.semaphore_wait(near_sem, 1)

        for step in range(2):

            @pl.when((core == 0) & (swaps[step] > 0))
            def _():
                signal(barrier, on_group(step))

    def await_far():
        @pl.when((core == 0) & (group > 0))
        def _():
            pl.semaphore_wait(barrier, 2)

        @pl.when((core == 0) & apart)
        def _():
            pl.semaphore_wait(far_sem, 2)

        @pl.when(core == 0)
        def _():
            signal(far_sem, sibling)

        for step in range(2):

            @pl.when((core == 0) & (swaps[step] == 0))
            def _():
                signal(far_sem, on_group(step))

        @pl.when(core == 1)
        def _():
            pl.semaphore_wait(far_sem, 1)

    def cot_copy(src, owner, half, slot, j):
        return remote(
            src, cots.at[rows_of(owner, TOKENS), columns(half)], cot_s, cot_r.at[slot], on_ring(j)
        )

    def cot_own(half, slot, j):
        return cot_copy(cots.at[own_rows, columns(half)], y, half, slot, j)

    def cot_passed(half, slot, j):
        owner = ring[RING - j]
        src = cots.at[rows_of(owner, TOKENS), columns(half)]
        return cot_copy(src, owner, half, slot, j)

    cot_copies = [
        cot_own(0, 0, 1),
        cot_own(1, 1, RING - 1),
        cot_own(1, 2, 1),
        cot_own(0, 3, RING - 1),
    ]
    cot_relays = [cot_passed(0, 4, 1), cot_passed(1, 5, RING - 1)]
    def act_copy(k, part, j):
        if k == 0:
            start = pl.multiple_of(ring[j] * SPAN + order[0] * ROWS + part * HALF, HALF)
            src, dst = pl.ds(start, HALF), pl.ds(part * HALF, HALF)
        else:
            src, dst = features(ring[j], order[k]), pl.ds(0, ROWS)
        return remote(
            act.at[:, src], acts.at[k, own_rows, dst], act_s, act_r.at[k + part], on_ring(j)
        )

    act_parts = [(0, 0), (0, 1), (1, 1), (2, 1), (3, 1)]
    act_copies = [[act_copy(k, part, j) for j in range(1, RING)] for k, part in act_parts]
    a_copies = [
        remote(
            rounded.at[rows_of(chip[j], CHUNK)],
            got_a.at[j],
            a_s,
            a_r,
            on_chip(j),
        )
        for j in range(1, CHIPS)
    ]
    def b_copy(step, slot, to):
        where = {"replica": to * CHIPS + m}
        return remote(sent_b.at[step], got_b.at[slot], b_s, b_r.at[slot], where)

    d_copies = [
        remote(total.at[m], total.at[m], d_s, d_r, on_chip(j)) for j in range(1, CHIPS)
    ]

    def w_copy(block, half, way, to):
        rows = scaled.at[block, pl.ds(half * HALF, HALF)]
        return remote(rows, rows, w_s, w_r.at[block, half], on_line(to))

    def part_copy(k, half, way, to):
        slot = part_slot(way, order[k], to)
        return remote(
            relay.at[k, half], landed.at[slot, half], part_s, part_r.at[slot, half], on_line(to)
        )

    def part_slot(way, block, at):
        return jnp.where(block == at, LINE, block) if way == 1 else block

    def part_wait(way, block, half):
        slot = part_slot(way, block, p)
        await_bytes(landed.at[slot, half], part_r.at[slot, half])
        return landed[slot, half].astype(F32)

    def back_copy(i, j):
        return remote(
            back.at[i, rows_of(ring[j], TOKENS)],
            grad_out.at[:, features(y, near[i])],
            back_s,
            back_r,
            on_ring(j),
        )

    def back_own(i):
        return pltpu.make_async_copy(
            back.at[i, own_rows], grad_out.at[:, features(y, near[i])], out_sem
        )

    def w_start(half):
        @pl.when(has_low)
        def _():
            w_copy(p, half, 1, p - 1).start()

        @pl.when(has_high)
        def _():
            w_copy(p, half, 0, p + 1).start()

    later = apart & (core == 1)

    @pl.when(jnp.logical_not(later))
    def _():
        for copy in a_copies:
            copy.start()

    for half in range(2):
        w_start(half)
    for copy in cot_copies + act_copies[0]:
        copy.start()

    @pl.when(later)
    def _():
        pl.semaphore_wait(near_sem, 1)
        for copy in a_copies:
            copy.start()


    def pass_near(half):
        @pl.when(inner)
        def _():
            w_copy(p - 1, half, 0, p + 1).wait_recv()
            w_copy(p - 1, half, 0, p + 1).start()
            w_copy(p + 1, half, 1, p - 1).wait_recv()
            w_copy(p + 1, half, 1, p - 1).start()

    def pass_far(half):
        @pl.when(p == 1)
        def _():
            w_copy(3, half, 1, 0).wait_recv()
            w_copy(3, half, 1, 0).start()

        @pl.when(p == 2)
        def _():
            w_copy(0, half, 0, 3).wait_recv()
            w_copy(0, half, 0, 3).start()

    def at_end_wait(block):
        @pl.when(edge)
        def _():
            for half in range(2):
                w_copy(block, half, 0, p).wait_recv()

    def input_grad(i):
        with jax.named_scope("ig%d" % i):
            if i > 0:
                at_end_wait(near[i])
            back[i] = lax.dot_general(
                cots[...],
                scaled[near[i]],
                (((1,), (1,)), ((), ())),
                preferred_element_type=F32,
            ).astype(BF16)
            for j in range(1, RING):
                back_copy(i, j).start()
            back_own(i).start()

    def rows(half):
        return pl.ds(half * HALF, HALF)

    def product(k, half):
        partial[k, rows(half)] = lax.dot_general(
            acts[k, :, rows(half)],
            cots[...],
            (((0,), (0,)), ((), ())),
            preferred_element_type=F32,
        )
        if k == LINE - 1:
            return

        @pl.when(edge)
        def _():
            relay[k, half] = partial[k, rows(half)].astype(BF16)

        @pl.when(p == 0)
        def _():
            part_copy(k, half, 0, 1).start()

        @pl.when(p == LINE - 1)
        def _():
            part_copy(k, half, 1, LINE - 2).start()

    others = pl.ds(0, (RING - 1) * TOKENS)

    def cot_wait(slot):
        await_bytes(cots.at[pl.ds(0, TOKENS), columns(0)], cot_r.at[slot])

    def act_wait(k, part=1):
        width = HALF if k == 0 else ROWS
        await_bytes(acts.at[k, others, pl.ds(0, width)], act_r.at[k + part])

    def gradient(k):
        with jax.named_scope("grad%d" % k):
            act_wait(k)
            product(k, 0)
            product(k, 1)

    def pass_part(k, half):
        def onward(way, to):
            both = partial[k, rows(half)] + part_wait(way, order[k], half)
            relay[k, half] = both.astype(BF16)
            part_copy(k, half, way, to).start()

        with jax.named_scope("part%d%d" % (k, half)):

            @pl.when(inner & (order[k] > p))
            def _():
                onward(0, p + 1)

            @pl.when(inner & (order[k] < p))
            def _():
                onward(1, p - 1)

    def outer_add(slot):
        b_copy(0, slot, swaps[0]).wait_recv()
        sum_a[...] += got_b[slot].astype(F32)

    def outer_step(step):
        if step == 0:
            await_far()
            b_copy(0, 0, swaps[0]).start()

        elif step == 1:
            outer_add(0)
            sent_b[1] = sum_a[...].astype(BF16)
            b_copy(1, 1, swaps[1]).start()

        else:

            outer_add(1)
            total[m] = sum_a[...].astype(BF16)
            for copy in d_copies:
                copy.start()

    late = group > 1

    inside0 = inner & (core == 0)
    spots = (True, edge, inner, p == 0, has_low, core == 0, core == 1, inside0)
    spots += (jnp.logical_not(inside0),)

    def outer_at(place):
        with jax.named_scope("outer_%d" % place):
            for member, step, where in SWAPS_AT[place]:

                @pl.when((group == member) & spots[where])
                def _():
                    outer_step(step)

    with jax.named_scope("cot_relay"):
        for slot in range(2):
            cot_wait(slot)
            cot_relays[slot].start()
    for copies in act_copies[1:]:
        for copy in copies:
            copy.start()
    with jax.named_scope("sum_a"):
        await_bytes(got_a.at[pl.ds(1, CHIPS - 1)], a_r)
        own_sum = weights[rows_of(m, CHUNK)]
        for j in range(1, CHIPS):
            own_sum += got_a[j].astype(F32)
        sum_a[...] = own_sum
        sent_b[0] = own_sum.astype(BF16)
    outer_at(0)
    with jax.named_scope("pass_near0"):
        pass_near(0)
    outer_at(1)
    with jax.named_scope("pass_near1"):
        pass_near(1)
    outer_at(2)
    with jax.named_scope("grad00"):
        await_bytes(scaled.at[0], local_sem.at[2])
        for slot in range(2, 6):
            cot_wait(slot)
        act_wait(0, 0)
        product(0, 0)
    with jax.named_scope("grad01"):
        act_wait(0, 1)
        product(0, 1)
    outer_at(3)
    with jax.named_scope("pass_far0"):
        pass_far(0)
    input_grad(0)
    with jax.named_scope("pass_far1"):
        pass_far(1)
    outer_at(4)
    pass_part(0, 0)
    input_grad(1)
    gradient(1)
    pass_part(0, 1)
    outer_at(5)
    gradient(2)
    input_grad(2)

    @pl.when(inner)
    def _():
        input_grad(3)

    outer_at(6)
    pass_part(2, 0)
    pass_part(1, 0)
    outer_at(7)
    gradient(3)
    pass_part(2, 1)
    outer_at(8)
    pass_part(1, 1)

    @pl.when(edge)
    def _():
        input_grad(3)

    with jax.named_scope("outer"):
        await_bytes(scaled.at[pl.ds(0, 3)], local_sem.at[3])
        loads[-1].wait()
        await_bytes(total.at[pl.ds(0, CHIPS - 1)], d_r)
        mean = total[...].astype(F32).reshape(ROWS, KVW) * (1.0 / REPLICAS)
        old = state[0].astype(F32)
        outer_grad = old - mean
        moment = OUTER_MOMENT * state[1].astype(F32) + outer_grad
        new = old - OUTER_RATE * (outer_grad + OUTER_MOMENT * moment)
        kept = MIXING * (1.0 - INNER_RATE * WEIGHT_DECAY)
        mixed[...] = kept * weights[...] + (1.0 - MIXING) * new

    for half in range(2):
        cut = rows(half)
        with jax.named_scope("last%d" % half):

            @pl.when(has_low)
            def _():
                partial[3, cut] += part_wait(0, p, half)

            @pl.when(has_high)
            def _():
                partial[3, cut] += part_wait(1, p, half)

            gradient_now = partial[3, cut] * FACTOR
            moment = BETA_FIRST * state[2, cut].astype(F32) + (1.0 - BETA_FIRST) * gradient_now
            spread = (
                BETA_SECOND * seconds[cut] + (1.0 - BETA_SECOND) * gradient_now * gradient_now
            )
            step = moment / (jnp.sqrt(spread) + EPSILON)
            first_out[cut] = moment
            merged_out[cut] = mixed[cut] - (MIXING * INNER_RATE) * step

    with jax.named_scope("drain_back"):
        three = landed.at[pl.ds(0, 3)]
        await_bytes(three, back_r)
    with jax.named_scope("drain"):
        await_bytes(scaled.at[0], out_sem)
        await_bytes(three, back_s)
        await_bytes(three, act_s)
        await_bytes(three, part_s)
        await_bytes(landed.at[pl.ds(0, 3), 0], cot_s)
        await_bytes(got_a.at[pl.ds(1, CHIPS - 1)], a_s)
        await_bytes(total.at[pl.ds(0, CHIPS - 1)], d_s)
        await_bytes(sent_b, b_s)

        @pl.when(edge)
        def _():
            await_bytes(scaled.at[0], w_s)

        @pl.when(inner)
        def _():
            await_bytes(landed, w_s)


def write_out(merged, first, grad, merged_out, first_out, grad_out, sem):
    copies = []
    for src, dst in ((grad, grad_out), (merged, merged_out), (first, first_out)):
        size = src.shape[0] // PIECES
        for i in range(PIECES):
            cut = pl.ds(i * size, size)
            copies.append(pltpu.make_async_copy(src.at[cut], dst.at[cut], sem.at[len(copies)]))
    for copy in copies:
        copy.start()
    for copy in copies:
        copy.wait()


def on_device(activations, cotangent, params, first_moment, second_moment, anchor, outer_momentum):
    any_spec = pl.BlockSpec(memory_space=pl.ANY)
    vmem_spec = pl.BlockSpec(memory_space=pltpu.VMEM)
    dma = pltpu.SemaphoreType.DMA
    results = (
        jax.ShapeDtypeStruct((ROWS, KVW), F32),
        jax.ShapeDtypeStruct((ROWS, KVW), F32),
        jax.ShapeDtypeStruct((TOKENS, D), BF16),
    )
    held = pl.pallas_call(
        kernel,
        out_shape=tuple(pltpu.VMEM(r.shape, r.dtype) for r in results),
        in_specs=[any_spec] * 7,
        out_specs=(vmem_spec,) * 3,
        scratch_shapes=[
            pltpu.VMEM((LINE, RING * TOKENS, ROWS), BF16),
            pltpu.VMEM((RING * TOKENS, KVW), BF16),
            pltpu.VMEM((LINE, ROWS, KVW), BF16),
            pltpu.VMEM((LINE, ROWS, KVW), F32),
            pltpu.VMEM((LINE + 1, 2, HALF, KVW), BF16),
            pltpu.VMEM((LINE - 1, 2, HALF, KVW), BF16),
            pltpu.VMEM((LINE, RING * TOKENS, ROWS), BF16),
            pltpu.VMEM((ROWS, KVW), F32),
            pltpu.VMEM((3, ROWS, KVW), BF16),
            pltpu.VMEM((ROWS, KVW), F32),
            pltpu.VMEM((ROWS, KVW), F32),
            pltpu.VMEM((ROWS, KVW), BF16),
            pltpu.VMEM((CHIPS, CHUNK, KVW), BF16),
            pltpu.VMEM((CHUNK, KVW), F32),
            pltpu.VMEM((2, CHUNK, KVW), BF16),
            pltpu.VMEM((3, CHUNK, KVW), BF16),
            pltpu.VMEM((CHIPS, CHUNK, KVW), BF16),
            pltpu.SemaphoreType.REGULAR,
            pltpu.SemaphoreType.REGULAR,
            dma((5,)),
            dma,
            dma((6,)),
            dma,
            dma((LINE + 1,)),
            dma,
            dma((LINE, 2)),
            dma,
            dma((LINE + 1, 2)),
            dma,
            dma,
            dma,
            dma,
            dma,
            dma((3,)),
            dma,
            dma,
            dma,
        ],
        compiler_params=pltpu.CompilerParams(
            collective_id=0, has_side_effects=True, vmem_limit_bytes=58 * 2**20
        ),
        name="diloco_step",
    )(
        activations[0, 0],
        cotangent[0, 0],
        params[0],
        first_moment[0],
        second_moment[0],
        anchor,
        outer_momentum,
    )
    merged, first, grad = pl.pallas_call(
        write_out,
        out_shape=results,
        in_specs=[vmem_spec] * 3,
        out_specs=(any_spec,) * 3,
        scratch_shapes=[dma((3 * PIECES,))],
        name="write_out",
    )(*(pltpu.with_memory_space_constraint(x, pltpu.VMEM) for x in held))
    return merged[None], first[None], grad[None, None]


def solution(mesh):
    placed = (
        P("replica", None, "fsdp", None),
        P("replica", None, "fsdp", None),
        P("replica", "fsdp", None),
        P("replica", "fsdp", None),
        P("replica", "fsdp", None),
        P("fsdp", None),
        P("fsdp", None),
    )
    return jax.shard_map(
        on_device,
        mesh=mesh,
        in_specs=placed,
        out_specs=(
            P("replica", "fsdp", None),
            P("replica", "fsdp", None),
            P("replica", None, "fsdp", None),
        ),
        check_vma=False,
    )
```

```python
import jax
import jax.numpy as jnp
from jax import lax
from jax.experimental import pallas as pl
from jax.experimental.pallas import tpu as pltpu
from jax.sharding import PartitionSpec as P

D = 4096
KVW = 512
ROWS = 256
TOKENS = 128
RING = 4
LINE = 4
GROUPS = 4
SPAN = ROWS * LINE
HALF = ROWS // 2
WIDE = KVW // 2
CHIPS = 8
CHUNK = ROWS // CHIPS
REPLICAS = 32
PIECES = 1

BETA_FIRST = 0.9
BETA_SECOND = 0.95
EPSILON = 1e-08
WEIGHT_DECAY = 0.1
INNER_RATE = 0.03
OUTER_RATE = 0.7
OUTER_MOMENT = 0.9
MIXING = 0.5

FACTOR = float(D) ** (-0.5)
ALL, ENDS, INSIDE, FOOT, ABOVE, CORE0, CORE1, INSIDE0, REST = range(9)
SWAPS_AT = (
    ((2, 0, ALL), (3, 0, ALL)),
    ((1, 0, ALL),),
    ((3, 1, FOOT),),
    ((2, 1, ALL), (3, 1, ABOVE)),
    ((0, 0, CORE0),),
    ((0, 0, CORE1), (1, 1, ALL), (0, 1, ENDS)),
    ((0, 1, INSIDE),),
    ((2, 2, ALL), (3, 2, ALL), (1, 2, ALL), (0, 2, INSIDE0)),
    ((0, 2, REST),),
)
MESH = pl.DeviceIdType.MESH
BF16 = jnp.bfloat16
F32 = jnp.float32


def kernel(
    act,
    cot,
    params,
    first,
    second,
    anchor,
    outer,
    merged_out,
    first_out,
    grad_out,
    acts,
    cots,
    scaled,
    partial,
    landed,
    relay,
    back,
    weights,
    state,
    seconds,
    mixed,
    rounded,
    got_a,
    sum_a,
    sent_b,
    got_b,
    total,
    near_sem,
    far_sem,
    local_sem,
    cot_s,
    cot_r,
    act_s,
    act_r,
    w_s,
    w_r,
    part_s,
    part_r,
    back_s,
    back_r,
    a_s,
    a_r,
    b_s,
    b_r,
    d_s,
    d_r,
    out_sem,
):
    replica = lax.axis_index("replica")
    shard = lax.axis_index("fsdp")
    y, p = shard // LINE, shard % LINE
    group, m = replica // CHIPS, replica % CHIPS
    core = replica % 2
    edge = (p == 0) | (p == LINE - 1)
    inner = (p == 1) | (p == 2)
    has_low, has_high = p > 0, p < LINE - 1
    upper = p // 2

    def mirrored(at):
        return at + upper * (LINE - 1 - 2 * at)

    is_end = 1 - (p + 1) % LINE // 2
    order = [mirrored(3), mirrored(2), mirrored(is_end), p]
    near = [p, mirrored(is_end), mirrored(2), mirrored(3)]
    ring = [lax.rem(y + j, RING) for j in range(RING)]
    chip = [lax.rem(m + j, CHIPS) for j in range(CHIPS)]
    swaps = [group + 1 - 2 * (group % 2), GROUPS - 1 - group]

    def on_ring(j):
        return {"fsdp": ring[j] * LINE + p}

    def on_line(at):
        return {"fsdp": y * LINE + at}

    def on_chip(j):
        return {"replica": group * CHIPS + chip[j]}

    def on_group(step):
        return {"replica": swaps[step] * CHIPS + m}

    def remote(src, dst, send, recv, where):
        return pltpu.make_async_remote_copy(
            src_ref=src,
            dst_ref=dst,
            send_sem=send,
            recv_sem=recv,
            device_id=where,
            device_id_type=MESH,
        )

    def rows_of(at, size):
        return pl.ds(pl.multiple_of(at * size, size), size)

    def features(ring_at, line_at):
        return pl.ds(pl.multiple_of(ring_at * SPAN + line_at * ROWS, ROWS), ROWS)

    def columns(half):
        return pl.ds(half * WIDE, WIDE)

    barrier = pltpu.get_barrier_semaphore()

    def signal(semaphore, where):
        pl.semaphore_signal(semaphore, inc=1, device_id=where, device_id_type=MESH)

    apart = group == 0
    hub = jnp.where(apart, 0, 1)
    hub_here = replica - core + hub
    sibling = {"replica": replica + 1 - 2 * core}
    near_gate = jnp.where(apart, replica, hub_here)
    for j in range(1, RING):
        signal(barrier, {"replica": near_gate, "fsdp": ring[j] * LINE + p})

    @pl.when(has_low)
    def _():
        signal(barrier, {"replica": near_gate, "fsdp": shard - 1})

    @pl.when(has_high)
    def _():
        signal(barrier, {"replica": near_gate, "fsdp": shard + 1})

    for j in range(2, CHIPS, 2):
        signal(barrier, {"replica": group * CHIPS + lax.rem(m - core + j, CHIPS) + hub})

    @pl.when(core != hub)
    def _():
        signal(barrier, sibling)

    own_rows = rows_of(y, TOKENS)
    first_load = pltpu.make_async_copy(params, weights, local_sem.at[0])
    first_load.start()
    loads = [pltpu.make_async_copy(cot, cots.at[own_rows], local_sem.at[1])]
    for k in range(LINE):
        loads.append(
            pltpu.make_async_copy(
                act.at[:, features(y, order[k])], acts.at[k, own_rows], local_sem.at[2]
            )
        )
    loads += [
        pltpu.make_async_copy(anchor, state.at[0], local_sem.at[3]),
        pltpu.make_async_copy(outer, state.at[1], local_sem.at[3]),
        pltpu.make_async_copy(first, state.at[2], local_sem.at[3]),
        pltpu.make_async_copy(second, seconds, local_sem.at[4]),
    ]
    for load in loads:
        load.start()

    def await_bytes(like, semaphore):
        pltpu.make_async_copy(like, like, semaphore).wait()

    with jax.named_scope("scale"):
        first_load.wait()
        scaled[p] = (weights[...] * FACTOR).astype(BF16)
        rounded[...] = weights[...].astype(BF16)

    loads[0].wait()
    with jax.named_scope("gate"):

        of_ring = (RING - 1) + (2 - is_end)
        of_chips = (CHIPS - 2) + 1
        met = jnp.where(apart, of_ring + (1 - core) * of_chips, 2 * of_ring + of_chips)

        @pl.when(apart | (core == 1))
        def _():
            pl.semaphore_wait(barrier, met)

        @pl.when(core == hub)
        def _():
            signal(near_sem, sibling)

        @pl.when((core == 0) & (group > 0))
        def _():
            pl.semaphore_wait(near_sem, 1)

        for step in range(2):

            @pl.when((core == 0) & (swaps[step] > 0))
            def _():
                signal(barrier, on_group(step))

    def await_far():
        @pl.when((core == 0) & (group > 0))
        def _():
            pl.semaphore_wait(barrier, 2)

        @pl.when((core == 0) & apart)
        def _():
            pl.semaphore_wait(far_sem, 2)

        @pl.when(core == 0)
        def _():
            signal(far_sem, sibling)

        for step in range(2):

            @pl.when((core == 0) & (swaps[step] == 0))
            def _():
                signal(far_sem, on_group(step))

        @pl.when(core == 1)
        def _():
            pl.semaphore_wait(far_sem, 1)

    def cot_copy(src, owner, half, slot, j):
        return remote(
            src, cots.at[rows_of(owner, TOKENS), columns(half)], cot_s, cot_r.at[slot], on_ring(j)
        )

    def cot_own(half, slot, j):
        return cot_copy(cots.at[own_rows, columns(half)], y, half, slot, j)

    def cot_passed(half, slot, j):
        owner = ring[RING - j]
        src = cots.at[rows_of(owner, TOKENS), columns(half)]
        return cot_copy(src, owner, half, slot, j)

    cot_copies = [
        cot_own(0, 0, 1),
        cot_own(1, 1, RING - 1),
        cot_own(1, 2, 1),
        cot_own(0, 3, RING - 1),
    ]
    cot_relays = [cot_passed(0, 4, 1), cot_passed(1, 5, RING - 1)]
    def act_copy(k, part, j):
        if k == 0:
            start = pl.multiple_of(ring[j] * SPAN + order[0] * ROWS + part * HALF, HALF)
            src, dst = pl.ds(start, HALF), pl.ds(part * HALF, HALF)
        else:
            src, dst = features(ring[j], order[k]), pl.ds(0, ROWS)
        return remote(
            act.at[:, src], acts.at[k, own_rows, dst], act_s, act_r.at[k + part], on_ring(j)
        )

    act_parts = [(0, 0), (0, 1), (1, 1), (2, 1), (3, 1)]
    act_copies = [[act_copy(k, part, j) for j in range(1, RING)] for k, part in act_parts]
    a_copies = [
        remote(
            rounded.at[rows_of(chip[j], CHUNK)],
            got_a.at[j],
            a_s,
            a_r,
            on_chip(j),
        )
        for j in range(1, CHIPS)
    ]
    def b_copy(step, slot, to):
        where = {"replica": to * CHIPS + m}
        return remote(sent_b.at[step], got_b.at[slot], b_s, b_r.at[slot], where)

    d_copies = [
        remote(total.at[m], total.at[m], d_s, d_r, on_chip(j)) for j in range(1, CHIPS)
    ]

    def w_copy(block, half, way, to):
        rows = scaled.at[block, pl.ds(half * HALF, HALF)]
        return remote(rows, rows, w_s, w_r.at[block, half], on_line(to))

    def part_copy(k, half, way, to):
        slot = part_slot(way, order[k], to)
        return remote(
            relay.at[k, half], landed.at[slot, half], part_s, part_r.at[slot, half], on_line(to)
        )

    def part_slot(way, block, at):
        return jnp.where(block == at, LINE, block) if way == 1 else block

    def part_wait(way, block, half):
        slot = part_slot(way, block, p)
        await_bytes(landed.at[slot, half], part_r.at[slot, half])
        return landed[slot, half].astype(F32)

    def back_copy(i, j):
        return remote(
            back.at[i, rows_of(ring[j], TOKENS)],
            grad_out.at[:, features(y, near[i])],
            back_s,
            back_r,
            on_ring(j),
        )

    def back_own(i):
        return pltpu.make_async_copy(
            back.at[i, own_rows], grad_out.at[:, features(y, near[i])], out_sem
        )

    def w_start(half):
        @pl.when(has_low)
        def _():
            w_copy(p, half, 1, p - 1).start()

        @pl.when(has_high)
        def _():
            w_copy(p, half, 0, p + 1).start()

    later = apart & (core == 1)

    @pl.when(jnp.logical_not(later))
    def _():
        for copy in a_copies:
            copy.start()

    for half in range(2):
        w_start(half)
    for copy in cot_copies + act_copies[0]:
        copy.start()

    @pl.when(later)
    def _():
        pl.semaphore_wait(near_sem, 1)
        for copy in a_copies:
            copy.start()


    def pass_near(half):
        @pl.when(inner)
        def _():
            w_copy(p - 1, half, 0, p + 1).wait_recv()
            w_copy(p - 1, half, 0, p + 1).start()
            w_copy(p + 1, half, 1, p - 1).wait_recv()
            w_copy(p + 1, half, 1, p - 1).start()

    def pass_far(half):
        @pl.when(p == 1)
        def _():
            w_copy(3, half, 1, 0).wait_recv()
            w_copy(3, half, 1, 0).start()

        @pl.when(p == 2)
        def _():
            w_copy(0, half, 0, 3).wait_recv()
            w_copy(0, half, 0, 3).start()

    def at_end_wait(block):
        @pl.when(edge)
        def _():
            for half in range(2):
                w_copy(block, half, 0, p).wait_recv()

    def input_grad(i):
        with jax.named_scope("ig%d" % i):
            if i > 0:
                at_end_wait(near[i])
            back[i] = lax.dot_general(
                cots[...],
                scaled[near[i]],
                (((1,), (1,)), ((), ())),
                preferred_element_type=F32,
            ).astype(BF16)
            for j in range(1, RING):
                back_copy(i, j).start()
            back_own(i).start()

    def rows(half):
        return pl.ds(half * HALF, HALF)

    def product(k, half):
        partial[k, rows(half)] = lax.dot_general(
            acts[k, :, rows(half)],
            cots[...],
            (((0,), (0,)), ((), ())),
            preferred_element_type=F32,
        )
        if k == LINE - 1:
            return

        @pl.when(edge)
        def _():
            relay[k, half] = partial[k, rows(half)].astype(BF16)

        @pl.when(p == 0)
        def _():
            part_copy(k, half, 0, 1).start()

        @pl.when(p == LINE - 1)
        def _():
            part_copy(k, half, 1, LINE - 2).start()

    others = pl.ds(0, (RING - 1) * TOKENS)

    def cot_wait(slot):
        await_bytes(cots.at[pl.ds(0, TOKENS), columns(0)], cot_r.at[slot])

    def act_wait(k, part=1):
        width = HALF if k == 0 else ROWS
        await_bytes(acts.at[k, others, pl.ds(0, width)], act_r.at[k + part])

    def gradient(k):
        with jax.named_scope("grad%d" % k):
            act_wait(k)
            product(k, 0)
            product(k, 1)

    def pass_part(k, half):
        def onward(way, to):
            both = partial[k, rows(half)] + part_wait(way, order[k], half)
            relay[k, half] = both.astype(BF16)
            part_copy(k, half, way, to).start()

        with jax.named_scope("part%d%d" % (k, half)):

            @pl.when(inner & (order[k] > p))
            def _():
                onward(0, p + 1)

            @pl.when(inner & (order[k] < p))
            def _():
                onward(1, p - 1)

    def outer_add(slot):
        b_copy(0, slot, swaps[0]).wait_recv()
        sum_a[...] += got_b[slot].astype(F32)

    def outer_step(step):
        if step == 0:
            await_far()
            b_copy(0, 0, swaps[0]).start()

        elif step == 1:
            outer_add(0)
            sent_b[1] = sum_a[...].astype(BF16)
            b_copy(1, 1, swaps[1]).start()

        else:

            outer_add(1)
            total[m] = sum_a[...].astype(BF16)
            for copy in d_copies:
                copy.start()

    late = group > 1

    inside0 = inner & (core == 0)
    spots = (True, edge, inner, p == 0, has_low, core == 0, core == 1, inside0)
    spots += (jnp.logical_not(inside0),)

    def outer_at(place):
        with jax.named_scope("outer_%d" % place):
            for member, step, where in SWAPS_AT[place]:

                @pl.when((group == member) & spots[where])
                def _():
                    outer_step(step)

    with jax.named_scope("cot_relay"):
        for slot in range(2):
            cot_wait(slot)
            cot_relays[slot].start()
    for copies in act_copies[1:]:
        for copy in copies:
            copy.start()
    with jax.named_scope("sum_a"):
        await_bytes(got_a.at[pl.ds(1, CHIPS - 1)], a_r)
        own_sum = weights[rows_of(m, CHUNK)]
        for j in range(1, CHIPS):
            own_sum += got_a[j].astype(F32)
        sum_a[...] = own_sum
        sent_b[0] = own_sum.astype(BF16)
    outer_at(0)
    with jax.named_scope("pass_near0"):
        pass_near(0)
    outer_at(1)
    with jax.named_scope("pass_near1"):
        pass_near(1)
    outer_at(2)
    with jax.named_scope("grad00"):
        await_bytes(scaled.at[0], local_sem.at[2])
        for slot in range(2, 6):
            cot_wait(slot)
        act_wait(0, 0)
        product(0, 0)
    with jax.named_scope("grad01"):
        act_wait(0, 1)
        product(0, 1)
    outer_at(3)
    with jax.named_scope("pass_far0"):
        pass_far(0)
    input_grad(0)
    with jax.named_scope("pass_far1"):
        pass_far(1)
    outer_at(4)
    pass_part(0, 0)
    input_grad(1)
    gradient(1)
    pass_part(0, 1)
    outer_at(5)
    gradient(2)
    input_grad(2)

    @pl.when(inner)
    def _():
        input_grad(3)

    outer_at(6)
    pass_part(2, 0)
    pass_part(1, 0)
    outer_at(7)
    gradient(3)
    pass_part(2, 1)
    outer_at(8)
    pass_part(1, 1)

    @pl.when(edge)
    def _():
        input_grad(3)

    of_mean = OUTER_RATE * (1.0 + OUTER_MOMENT)
    with jax.named_scope("base"):
        await_bytes(scaled.at[pl.ds(0, 3)], local_sem.at[3])
        loads[-1].wait()
        old = state[0].astype(F32)
        known = (1.0 - of_mean) * old - OUTER_RATE * OUTER_MOMENT**2 * state[1].astype(F32)
        kept = MIXING * (1.0 - INNER_RATE * WEIGHT_DECAY)
        mixed[...] = kept * weights[...] + (1.0 - MIXING) * known

    for half in range(2):
        cut = rows(half)
        with jax.named_scope("last%d" % half):

            @pl.when(has_low)
            def _():
                partial[3, cut] += part_wait(0, p, half)

            @pl.when(has_high)
            def _():
                partial[3, cut] += part_wait(1, p, half)

            gradient_now = partial[3, cut] * FACTOR
            moment = BETA_FIRST * state[2, cut].astype(F32) + (1.0 - BETA_FIRST) * gradient_now
            spread = BETA_SECOND * seconds[cut] + (1.0 - BETA_SECOND) * gradient_now * gradient_now
            step = moment / (jnp.sqrt(spread) + EPSILON)
            first_out[cut] = moment
            mixed[cut] -= (MIXING * INNER_RATE) * step

    with jax.named_scope("outer"):
        await_bytes(total.at[pl.ds(0, CHIPS - 1)], d_r)
        share = (1.0 - MIXING) * of_mean / REPLICAS
        merged_out[...] = mixed[...] + share * total[...].astype(F32).reshape(ROWS, KVW)

    with jax.named_scope("drain_back"):
        three = landed.at[pl.ds(0, 3)]
        await_bytes(three, back_r)
    with jax.named_scope("drain"):
        await_bytes(scaled.at[0], out_sem)
        await_bytes(three, back_s)
        await_bytes(three, act_s)
        await_bytes(three, part_s)
        await_bytes(landed.at[pl.ds(0, 3), 0], cot_s)
        await_bytes(got_a.at[pl.ds(1, CHIPS - 1)], a_s)
        await_bytes(total.at[pl.ds(0, CHIPS - 1)], d_s)
        await_bytes(sent_b, b_s)

        @pl.when(edge)
        def _():
            await_bytes(scaled.at[0], w_s)

        @pl.when(inner)
        def _():
            await_bytes(landed, w_s)


def write_out(merged, first, grad, merged_out, first_out, grad_out, sem):
    copies = []
    for src, dst in ((grad, grad_out), (merged, merged_out), (first, first_out)):
        size = src.shape[0] // PIECES
        for i in range(PIECES):
            cut = pl.ds(i * size, size)
            copies.append(pltpu.make_async_copy(src.at[cut], dst.at[cut], sem.at[len(copies)]))
    for copy in copies:
        copy.start()
    for copy in copies:
        copy.wait()


def on_device(activations, cotangent, params, first_moment, second_moment, anchor, outer_momentum):
    any_spec = pl.BlockSpec(memory_space=pl.ANY)
    vmem_spec = pl.BlockSpec(memory_space=pltpu.VMEM)
    dma = pltpu.SemaphoreType.DMA
    results = (
        jax.ShapeDtypeStruct((ROWS, KVW), F32),
        jax.ShapeDtypeStruct((ROWS, KVW), F32),
        jax.ShapeDtypeStruct((TOKENS, D), BF16),
    )
    held = pl.pallas_call(
        kernel,
        out_shape=tuple(pltpu.VMEM(r.shape, r.dtype) for r in results),
        in_specs=[any_spec] * 7,
        out_specs=(vmem_spec,) * 3,
        scratch_shapes=[
            pltpu.VMEM((LINE, RING * TOKENS, ROWS), BF16),
            pltpu.VMEM((RING * TOKENS, KVW), BF16),
            pltpu.VMEM((LINE, ROWS, KVW), BF16),
            pltpu.VMEM((LINE, ROWS, KVW), F32),
            pltpu.VMEM((LINE + 1, 2, HALF, KVW), BF16),
            pltpu.VMEM((LINE - 1, 2, HALF, KVW), BF16),
            pltpu.VMEM((LINE, RING * TOKENS, ROWS), BF16),
            pltpu.VMEM((ROWS, KVW), F32),
            pltpu.VMEM((3, ROWS, KVW), BF16),
            pltpu.VMEM((ROWS, KVW), F32),
            pltpu.VMEM((ROWS, KVW), F32),
            pltpu.VMEM((ROWS, KVW), BF16),
            pltpu.VMEM((CHIPS, CHUNK, KVW), BF16),
            pltpu.VMEM((CHUNK, KVW), F32),
            pltpu.VMEM((2, CHUNK, KVW), BF16),
            pltpu.VMEM((3, CHUNK, KVW), BF16),
            pltpu.VMEM((CHIPS, CHUNK, KVW), BF16),
            pltpu.SemaphoreType.REGULAR,
            pltpu.SemaphoreType.REGULAR,
            dma((5,)),
            dma,
            dma((6,)),
            dma,
            dma((LINE + 1,)),
            dma,
            dma((LINE, 2)),
            dma,
            dma((LINE + 1, 2)),
            dma,
            dma,
            dma,
            dma,
            dma,
            dma((3,)),
            dma,
            dma,
            dma,
        ],
        compiler_params=pltpu.CompilerParams(
            collective_id=0, has_side_effects=True, vmem_limit_bytes=58 * 2**20
        ),
        name="diloco_step",
    )(
        activations[0, 0],
        cotangent[0, 0],
        params[0],
        first_moment[0],
        second_moment[0],
        anchor,
        outer_momentum,
    )
    merged, first, grad = pl.pallas_call(
        write_out,
        out_shape=results,
        in_specs=[vmem_spec] * 3,
        out_specs=(any_spec,) * 3,
        scratch_shapes=[dma((3 * PIECES,))],
        name="write_out",
    )(*(pltpu.with_memory_space_constraint(x, pltpu.VMEM) for x in held))
    return merged[None], first[None], grad[None, None]


def solution(mesh):
    placed = (
        P("replica", None, "fsdp", None),
        P("replica", None, "fsdp", None),
        P("replica", "fsdp", None),
        P("replica", "fsdp", None),
        P("replica", "fsdp", None),
        P("fsdp", None),
        P("fsdp", None),
    )
    return jax.shard_map(
        on_device,
        mesh=mesh,
        in_specs=placed,
        out_specs=(
            P("replica", "fsdp", None),
            P("replica", "fsdp", None),
            P("replica", None, "fsdp", None),
        ),
        check_vma=False,
    )
```

```python
import jax
import jax.numpy as jnp
from jax import lax
from jax.experimental import pallas as pl
from jax.experimental.pallas import tpu as pltpu
from jax.sharding import PartitionSpec as P

D = 4096
KVW = 512
ROWS = 256
TOKENS = 128
RING = 4
LINE = 4
GROUPS = 4
SPAN = ROWS * LINE
HALF = ROWS // 2
WIDE = KVW // 2
CHIPS = 8
CHUNK = ROWS // CHIPS
REPLICAS = 32
PIECES = 1

BETA_FIRST = 0.9
BETA_SECOND = 0.95
EPSILON = 1e-08
WEIGHT_DECAY = 0.1
INNER_RATE = 0.03
OUTER_RATE = 0.7
OUTER_MOMENT = 0.9
MIXING = 0.5

FACTOR = float(D) ** (-0.5)
ALL, ENDS, INSIDE, FOOT, ABOVE, CORE0, CORE1, INSIDE0, REST = range(9)
SWAPS_AT = (
    ((2, 0, ALL), (3, 0, ALL)),
    ((1, 0, ALL),),
    ((3, 1, FOOT),),
    ((2, 1, ALL), (3, 1, ABOVE)),
    ((0, 0, CORE0),),
    ((0, 0, CORE1), (1, 1, ALL), (0, 1, ENDS)),
    ((0, 1, INSIDE),),
    ((2, 2, ALL), (3, 2, ALL), (1, 2, ALL), (0, 2, INSIDE0)),
    ((0, 2, REST),),
)
MESH = pl.DeviceIdType.MESH
BF16 = jnp.bfloat16
F32 = jnp.float32


def kernel(
    act,
    cot,
    params,
    first,
    second,
    anchor,
    outer,
    merged_out,
    first_out,
    grad_out,
    acts,
    cots,
    scaled,
    partial,
    landed,
    relay,
    back,
    weights,
    state,
    seconds,
    mixed,
    rounded,
    got_a,
    sum_a,
    sent_b,
    got_b,
    total,
    near_sem,
    far_sem,
    local_sem,
    cot_s,
    cot_r,
    act_s,
    act_r,
    w_s,
    w_r,
    part_s,
    part_r,
    back_s,
    back_r,
    a_s,
    a_r,
    b_s,
    b_r,
    d_s,
    d_r,
    out_sem,
):
    replica = lax.axis_index("replica")
    shard = lax.axis_index("fsdp")
    y, p = shard // LINE, shard % LINE
    group, m = replica // CHIPS, replica % CHIPS
    core = replica % 2
    edge = (p == 0) | (p == LINE - 1)
    inner = (p == 1) | (p == 2)
    has_low, has_high = p > 0, p < LINE - 1
    upper = p // 2

    def mirrored(at):
        return at + upper * (LINE - 1 - 2 * at)

    is_end = 1 - (p + 1) % LINE // 2
    order = [mirrored(3), mirrored(2), mirrored(is_end), p]
    near = [p, mirrored(is_end), mirrored(2), mirrored(3)]
    ring = [lax.rem(y + j, RING) for j in range(RING)]
    chip = [lax.rem(m + j, CHIPS) for j in range(CHIPS)]
    swaps = [group + 1 - 2 * (group % 2), GROUPS - 1 - group]

    def on_ring(j):
        return {"fsdp": ring[j] * LINE + p}

    def on_line(at):
        return {"fsdp": y * LINE + at}

    def on_chip(j):
        return {"replica": group * CHIPS + chip[j]}

    def on_group(step):
        return {"replica": swaps[step] * CHIPS + m}

    def remote(src, dst, send, recv, where):
        return pltpu.make_async_remote_copy(
            src_ref=src,
            dst_ref=dst,
            send_sem=send,
            recv_sem=recv,
            device_id=where,
            device_id_type=MESH,
        )

    def rows_of(at, size):
        return pl.ds(pl.multiple_of(at * size, size), size)

    def features(ring_at, line_at):
        return pl.ds(pl.multiple_of(ring_at * SPAN + line_at * ROWS, ROWS), ROWS)

    def columns(half):
        return pl.ds(half * WIDE, WIDE)

    barrier = pltpu.get_barrier_semaphore()

    def signal(semaphore, where):
        pl.semaphore_signal(semaphore, inc=1, device_id=where, device_id_type=MESH)

    apart = group == 0
    hub = jnp.where(apart, 0, 1)
    hub_here = replica - core + hub
    sibling = {"replica": replica + 1 - 2 * core}
    near_gate = jnp.where(apart, replica, hub_here)
    for j in range(1, RING):
        signal(barrier, {"replica": near_gate, "fsdp": ring[j] * LINE + p})

    @pl.when(has_low)
    def _():
        signal(barrier, {"replica": near_gate, "fsdp": shard - 1})

    @pl.when(has_high)
    def _():
        signal(barrier, {"replica": near_gate, "fsdp": shard + 1})

    for j in range(2, CHIPS, 2):
        signal(barrier, {"replica": group * CHIPS + lax.rem(m - core + j, CHIPS) + hub})

    @pl.when(core != hub)
    def _():
        signal(barrier, sibling)

    own_rows = rows_of(y, TOKENS)
    first_load = pltpu.make_async_copy(params, weights, local_sem.at[0])
    first_load.start()
    loads = [pltpu.make_async_copy(cot, cots.at[own_rows], local_sem.at[1])]
    for k in range(LINE):
        loads.append(
            pltpu.make_async_copy(
                act.at[:, features(y, order[k])], acts.at[k, own_rows], local_sem.at[2]
            )
        )
    loads += [
        pltpu.make_async_copy(anchor, state.at[0], local_sem.at[3]),
        pltpu.make_async_copy(outer, state.at[1], local_sem.at[3]),
        pltpu.make_async_copy(first, state.at[2], local_sem.at[3]),
        pltpu.make_async_copy(second, seconds, local_sem.at[4]),
    ]
    for load in loads:
        load.start()

    def await_bytes(like, semaphore):
        pltpu.make_async_copy(like, like, semaphore).wait()

    with jax.named_scope("scale"):
        first_load.wait()
        scaled[p] = (weights[...] * FACTOR).astype(BF16)
        rounded[...] = weights[...].astype(BF16)

    loads[0].wait()
    with jax.named_scope("gate"):

        of_ring = (RING - 1) + (2 - is_end)
        of_chips = (CHIPS - 2) + 1
        met = jnp.where(apart, of_ring + (1 - core) * of_chips, 2 * of_ring + of_chips)

        @pl.when(apart | (core == 1))
        def _():
            pl.semaphore_wait(barrier, met)

        @pl.when(core == hub)
        def _():
            signal(near_sem, sibling)

        @pl.when((core == 0) & (group > 0))
        def _():
            pl.semaphore_wait(near_sem, 1)

        for step in range(2):

            @pl.when((core == 0) & (swaps[step] > 0))
            def _():
                signal(barrier, on_group(step))

    def await_far():
        @pl.when((core == 0) & (group > 0))
        def _():
            pl.semaphore_wait(barrier, 2)

        @pl.when((core == 0) & apart)
        def _():
            pl.semaphore_wait(far_sem, 2)

        @pl.when(core == 0)
        def _():
            signal(far_sem, sibling)

        for step in range(2):

            @pl.when((core == 0) & (swaps[step] == 0))
            def _():
                signal(far_sem, on_group(step))

        @pl.when(core == 1)
        def _():
            pl.semaphore_wait(far_sem, 1)

    def cot_copy(src, owner, half, slot, j):
        return remote(
            src, cots.at[rows_of(owner, TOKENS), columns(half)], cot_s, cot_r.at[slot], on_ring(j)
        )

    def cot_own(half, slot, j):
        return cot_copy(cots.at[own_rows, columns(half)], y, half, slot, j)

    def cot_passed(half, slot, j):
        owner = ring[RING - j]
        src = cots.at[rows_of(owner, TOKENS), columns(half)]
        return cot_copy(src, owner, half, slot, j)

    cot_copies = [
        cot_own(0, 0, 1),
        cot_own(1, 1, RING - 1),
        cot_own(1, 2, 1),
        cot_own(0, 3, RING - 1),
    ]
    cot_relays = [cot_passed(0, 4, 1), cot_passed(1, 5, RING - 1)]
    def act_copy(k, part, j):
        if k == 0:
            start = pl.multiple_of(ring[j] * SPAN + order[0] * ROWS + part * HALF, HALF)
            src, dst = pl.ds(start, HALF), pl.ds(part * HALF, HALF)
        else:
            src, dst = features(ring[j], order[k]), pl.ds(0, ROWS)
        return remote(
            act.at[:, src], acts.at[k, own_rows, dst], act_s, act_r.at[k + part], on_ring(j)
        )

    act_parts = [(0, 0), (0, 1), (1, 1), (2, 1), (3, 1)]
    act_copies = [[act_copy(k, part, j) for j in range(1, RING)] for k, part in act_parts]
    a_copies = [
        remote(
            rounded.at[rows_of(chip[j], CHUNK)],
            got_a.at[j],
            a_s,
            a_r,
            on_chip(j),
        )
        for j in range(1, CHIPS)
    ]
    def b_copy(step, slot, to):
        where = {"replica": to * CHIPS + m}
        return remote(sent_b.at[step], got_b.at[slot], b_s, b_r.at[slot], where)

    d_copies = [
        remote(total.at[m], total.at[m], d_s, d_r, on_chip(j)) for j in range(1, CHIPS)
    ]

    def w_copy(block, half, way, to):
        rows = scaled.at[block, pl.ds(half * HALF, HALF)]
        return remote(rows, rows, w_s, w_r.at[block, half], on_line(to))

    def part_copy(k, half, way, to):
        slot = part_slot(way, order[k], to)
        return remote(
            relay.at[k, half], landed.at[slot, half], part_s, part_r.at[slot, half], on_line(to)
        )

    def part_slot(way, block, at):
        return jnp.where(block == at, LINE, block) if way == 1 else block

    def part_wait(way, block, half):
        slot = part_slot(way, block, p)
        await_bytes(landed.at[slot, half], part_r.at[slot, half])
        return landed[slot, half].astype(F32)

    def back_copy(i, j):
        return remote(
            back.at[i, rows_of(ring[j], TOKENS)],
            grad_out.at[:, features(y, near[i])],
            back_s,
            back_r,
            on_ring(j),
        )

    def back_own(i):
        return pltpu.make_async_copy(
            back.at[i, own_rows], grad_out.at[:, features(y, near[i])], out_sem
        )

    def w_start(half):
        @pl.when(has_low)
        def _():
            w_copy(p, half, 1, p - 1).start()

        @pl.when(has_high)
        def _():
            w_copy(p, half, 0, p + 1).start()

    later = apart & (core == 1)

    for copy in cot_copies:
        copy.start()

    @pl.when(jnp.logical_not(later))
    def _():
        for copy in a_copies:
            copy.start()

    for half in range(2):
        w_start(half)
    for copy in act_copies[0]:
        copy.start()

    @pl.when(later)
    def _():
        pl.semaphore_wait(near_sem, 1)
        for copy in a_copies:
            copy.start()


    def pass_near(half):
        @pl.when(inner)
        def _():
            w_copy(p - 1, half, 0, p + 1).wait_recv()
            w_copy(p - 1, half, 0, p + 1).start()
            w_copy(p + 1, half, 1, p - 1).wait_recv()
            w_copy(p + 1, half, 1, p - 1).start()

    def pass_far(half):
        @pl.when(p == 1)
        def _():
            w_copy(3, half, 1, 0).wait_recv()
            w_copy(3, half, 1, 0).start()

        @pl.when(p == 2)
        def _():
            w_copy(0, half, 0, 3).wait_recv()
            w_copy(0, half, 0, 3).start()

    def at_end_wait(block):
        @pl.when(edge)
        def _():
            for half in range(2):
                w_copy(block, half, 0, p).wait_recv()

    def input_grad(i):
        with jax.named_scope("ig%d" % i):
            if i > 0:
                at_end_wait(near[i])
            back[i] = lax.dot_general(
                cots[...],
                scaled[near[i]],
                (((1,), (1,)), ((), ())),
                preferred_element_type=F32,
            ).astype(BF16)
            for j in range(1, RING):
                back_copy(i, j).start()
            back_own(i).start()

    def rows(half):
        return pl.ds(half * HALF, HALF)

    def product(k, half):
        partial[k, rows(half)] = lax.dot_general(
            acts[k, :, rows(half)],
            cots[...],
            (((0,), (0,)), ((), ())),
            preferred_element_type=F32,
        )
        if k == LINE - 1:
            return

        @pl.when(edge)
        def _():
            relay[k, half] = partial[k, rows(half)].astype(BF16)

        @pl.when(p == 0)
        def _():
            part_copy(k, half, 0, 1).start()

        @pl.when(p == LINE - 1)
        def _():
            part_copy(k, half, 1, LINE - 2).start()

    others = pl.ds(0, (RING - 1) * TOKENS)

    def cot_wait(slot):
        await_bytes(cots.at[pl.ds(0, TOKENS), columns(0)], cot_r.at[slot])

    def act_wait(k, part=1):
        width = HALF if k == 0 else ROWS
        await_bytes(acts.at[k, others, pl.ds(0, width)], act_r.at[k + part])

    def gradient(k):
        with jax.named_scope("grad%d" % k):
            act_wait(k)
            product(k, 0)
            product(k, 1)

    def pass_part(k, half):
        def onward(way, to):
            both = partial[k, rows(half)] + part_wait(way, order[k], half)
            relay[k, half] = both.astype(BF16)
            part_copy(k, half, way, to).start()

        with jax.named_scope("part%d%d" % (k, half)):

            @pl.when(inner & (order[k] > p))
            def _():
                onward(0, p + 1)

            @pl.when(inner & (order[k] < p))
            def _():
                onward(1, p - 1)

    def outer_add(slot):
        b_copy(0, slot, swaps[0]).wait_recv()
        sum_a[...] += got_b[slot].astype(F32)

    def outer_step(step):
        if step == 0:
            await_far()
            b_copy(0, 0, swaps[0]).start()

        elif step == 1:
            outer_add(0)
            sent_b[1] = sum_a[...].astype(BF16)
            b_copy(1, 1, swaps[1]).start()

        else:

            outer_add(1)
            total[m] = sum_a[...].astype(BF16)
            for copy in d_copies:
                copy.start()

    late = group > 1

    inside0 = inner & (core == 0)
    spots = (True, edge, inner, p == 0, has_low, core == 0, core == 1, inside0)
    spots += (jnp.logical_not(inside0),)

    def outer_at(place):
        with jax.named_scope("outer_%d" % place):
            for member, step, where in SWAPS_AT[place]:

                @pl.when((group == member) & spots[where])
                def _():
                    outer_step(step)

    with jax.named_scope("cot_relay"):
        for slot in range(2):
            cot_wait(slot)
            cot_relays[slot].start()
    for copies in act_copies[1:]:
        for copy in copies:
            copy.start()
    with jax.named_scope("sum_a"):
        await_bytes(got_a.at[pl.ds(1, CHIPS - 1)], a_r)
        own_sum = weights[rows_of(m, CHUNK)]
        for j in range(1, CHIPS):
            own_sum += got_a[j].astype(F32)
        sum_a[...] = own_sum
        sent_b[0] = own_sum.astype(BF16)
    outer_at(0)
    with jax.named_scope("pass_near0"):
        pass_near(0)
    outer_at(1)
    with jax.named_scope("pass_near1"):
        pass_near(1)
    outer_at(2)
    with jax.named_scope("grad00"):
        await_bytes(scaled.at[0], local_sem.at[2])
        for slot in range(2, 6):
            cot_wait(slot)
        act_wait(0, 0)
        product(0, 0)
    with jax.named_scope("grad01"):
        act_wait(0, 1)
        product(0, 1)
    outer_at(3)
    with jax.named_scope("pass_far0"):
        pass_far(0)
    input_grad(0)
    with jax.named_scope("pass_far1"):
        pass_far(1)
    outer_at(4)
    pass_part(0, 0)
    input_grad(1)
    gradient(1)
    pass_part(0, 1)
    outer_at(5)
    gradient(2)
    input_grad(2)

    @pl.when(inner)
    def _():
        input_grad(3)

    outer_at(6)
    pass_part(2, 0)
    pass_part(1, 0)
    outer_at(7)
    gradient(3)
    pass_part(2, 1)
    outer_at(8)
    pass_part(1, 1)

    @pl.when(edge)
    def _():
        input_grad(3)

    of_mean = OUTER_RATE * (1.0 + OUTER_MOMENT)
    with jax.named_scope("base"):
        await_bytes(scaled.at[pl.ds(0, 3)], local_sem.at[3])
        loads[-1].wait()
        old = state[0].astype(F32)
        known = (1.0 - of_mean) * old - OUTER_RATE * OUTER_MOMENT**2 * state[1].astype(F32)
        kept = MIXING * (1.0 - INNER_RATE * WEIGHT_DECAY)
        mixed[...] = kept * weights[...] + (1.0 - MIXING) * known

    for half in range(2):
        cut = rows(half)
        with jax.named_scope("last%d" % half):

            @pl.when(has_low)
            def _():
                partial[3, cut] += part_wait(0, p, half)

            @pl.when(has_high)
            def _():
                partial[3, cut] += part_wait(1, p, half)

            gradient_now = partial[3, cut] * FACTOR
            moment = BETA_FIRST * state[2, cut].astype(F32) + (1.0 - BETA_FIRST) * gradient_now
            spread = BETA_SECOND * seconds[cut] + (1.0 - BETA_SECOND) * gradient_now * gradient_now
            step = moment / (jnp.sqrt(spread) + EPSILON)
            first_out[cut] = moment
            mixed[cut] -= (MIXING * INNER_RATE) * step

    with jax.named_scope("outer"):
        await_bytes(total.at[pl.ds(0, CHIPS - 1)], d_r)
        share = (1.0 - MIXING) * of_mean / REPLICAS
        merged_out[...] = mixed[...] + share * total[...].astype(F32).reshape(ROWS, KVW)

    with jax.named_scope("drain_back"):
        three = landed.at[pl.ds(0, 3)]
        await_bytes(three, back_r)
    with jax.named_scope("drain"):
        await_bytes(scaled.at[0], out_sem)
        await_bytes(three, back_s)
        await_bytes(three, act_s)
        await_bytes(three, part_s)
        await_bytes(landed.at[pl.ds(0, 3), 0], cot_s)
        await_bytes(got_a.at[pl.ds(1, CHIPS - 1)], a_s)
        await_bytes(total.at[pl.ds(0, CHIPS - 1)], d_s)
        await_bytes(sent_b, b_s)

        @pl.when(edge)
        def _():
            await_bytes(scaled.at[0], w_s)

        @pl.when(inner)
        def _():
            await_bytes(landed, w_s)


def write_out(merged, first, grad, merged_out, first_out, grad_out, sem):
    copies = []
    for src, dst in ((grad, grad_out), (merged, merged_out), (first, first_out)):
        size = src.shape[0] // PIECES
        for i in range(PIECES):
            cut = pl.ds(i * size, size)
            copies.append(pltpu.make_async_copy(src.at[cut], dst.at[cut], sem.at[len(copies)]))
    for copy in copies:
        copy.start()
    for copy in copies:
        copy.wait()


def on_device(activations, cotangent, params, first_moment, second_moment, anchor, outer_momentum):
    any_spec = pl.BlockSpec(memory_space=pl.ANY)
    vmem_spec = pl.BlockSpec(memory_space=pltpu.VMEM)
    dma = pltpu.SemaphoreType.DMA
    results = (
        jax.ShapeDtypeStruct((ROWS, KVW), F32),
        jax.ShapeDtypeStruct((ROWS, KVW), F32),
        jax.ShapeDtypeStruct((TOKENS, D), BF16),
    )
    held = pl.pallas_call(
        kernel,
        out_shape=tuple(pltpu.VMEM(r.shape, r.dtype) for r in results),
        in_specs=[any_spec] * 7,
        out_specs=(vmem_spec,) * 3,
        scratch_shapes=[
            pltpu.VMEM((LINE, RING * TOKENS, ROWS), BF16),
            pltpu.VMEM((RING * TOKENS, KVW), BF16),
            pltpu.VMEM((LINE, ROWS, KVW), BF16),
            pltpu.VMEM((LINE, ROWS, KVW), F32),
            pltpu.VMEM((LINE + 1, 2, HALF, KVW), BF16),
            pltpu.VMEM((LINE - 1, 2, HALF, KVW), BF16),
            pltpu.VMEM((LINE, RING * TOKENS, ROWS), BF16),
            pltpu.VMEM((ROWS, KVW), F32),
            pltpu.VMEM((3, ROWS, KVW), BF16),
            pltpu.VMEM((ROWS, KVW), F32),
            pltpu.VMEM((ROWS, KVW), F32),
            pltpu.VMEM((ROWS, KVW), BF16),
            pltpu.VMEM((CHIPS, CHUNK, KVW), BF16),
            pltpu.VMEM((CHUNK, KVW), F32),
            pltpu.VMEM((2, CHUNK, KVW), BF16),
            pltpu.VMEM((3, CHUNK, KVW), BF16),
            pltpu.VMEM((CHIPS, CHUNK, KVW), BF16),
            pltpu.SemaphoreType.REGULAR,
            pltpu.SemaphoreType.REGULAR,
            dma((5,)),
            dma,
            dma((6,)),
            dma,
            dma((LINE + 1,)),
            dma,
            dma((LINE, 2)),
            dma,
            dma((LINE + 1, 2)),
            dma,
            dma,
            dma,
            dma,
            dma,
            dma((3,)),
            dma,
            dma,
            dma,
        ],
        compiler_params=pltpu.CompilerParams(
            collective_id=0, has_side_effects=True, vmem_limit_bytes=58 * 2**20
        ),
        name="diloco_step",
    )(
        activations[0, 0],
        cotangent[0, 0],
        params[0],
        first_moment[0],
        second_moment[0],
        anchor,
        outer_momentum,
    )
    merged, first, grad = pl.pallas_call(
        write_out,
        out_shape=results,
        in_specs=[vmem_spec] * 3,
        out_specs=(any_spec,) * 3,
        scratch_shapes=[dma((3 * PIECES,))],
        name="write_out",
    )(*(pltpu.with_memory_space_constraint(x, pltpu.VMEM) for x in held))
    return merged[None], first[None], grad[None, None]


def solution(mesh):
    placed = (
        P("replica", None, "fsdp", None),
        P("replica", None, "fsdp", None),
        P("replica", "fsdp", None),
        P("replica", "fsdp", None),
        P("replica", "fsdp", None),
        P("fsdp", None),
        P("fsdp", None),
    )
    return jax.shard_map(
        on_device,
        mesh=mesh,
        in_specs=placed,
        out_specs=(
            P("replica", "fsdp", None),
            P("replica", "fsdp", None),
            P("replica", None, "fsdp", None),
        ),
        check_vma=False,
    )
```
